256 devices in a mesh: dp: 32 (over y_lo, z, core), ctx: 8 (over y_hi, x).
Axes of the slice: x: 4, y: 4 (y_hi: 2, y_lo: 2; y = y_hi * 2 + y_lo), z: 8, core: 2. Of those that a mesh axis runs over, the one named last changes fastest.
Arguments:
- queries: bfloat16 [32, 1024, 4096], P('dp', 'ctx'), may hold values from -5 to 5
- key_vectors: bfloat16 [32, 1024, 512], P('dp', 'ctx'), may hold values from -5 to 5
- activations: bfloat16 [32, 1024, 4096], P('dp', 'ctx'), may hold values from -6 to 6
- value_weight: bfloat16 [4096, 512], P(('dp', 'ctx')), may hold values from -0.09375 to 0.09375
- attended_grad: bfloat16 [32, 1024, 4096], P('dp', 'ctx'), may hold values from -6 to 6
- doc_ids: int32 [32, 1024], P('dp'), may hold values from 0 to 15, never falling along the last dimension, each value on 1 to 512 neighbouring positions
- shard_plan: int32 [32, 32], P('dp'), may hold values from 0 to 31, as said below
- round_bits: int32 [8, 1024, 8], replicated, may hold values from 0 to 1073741823
Outputs:
- attended: bfloat16 [32, 1024, 4096], P('dp', 'ctx')
- query_grad: bfloat16 [32, 1024, 4096], P('dp', 'ctx')
- key_grad: bfloat16 [32, 1024, 512], P('dp', 'ctx')
- weight_grad: float32 [4096, 512], P(('dp', 'ctx'))
The draws below stay inside these ranges and needn't reach their ends.
Inputs may be any that keep to these rules, and one draw needn't show every extreme that they name: Each row is a permutation of the 32 blocks; index d of ctx holds the places of blocks shard_plan[s, d * 4] to shard_plan[s, d * 4 + 3] in this order, and of these at most 1 come from any one index of ctx (block b comes from index b // 4), a bound reached in every row.
All inputs are finite; a program needn't handle non-finite values.
Results may differ from the reference program's by a relative error of at most 0.022.
Values may be sent and summed in bfloat16 or wider, within the bound.
A program may use at most 192 MiB of HBM per device.

```python
import math
import jax
import jax.numpy as jnp
import numpy as np
from jax import lax

D = 4096
HEADS = 32
KV_HEADS = 4
HEAD_DIM = 128
BPD = 4
TOK_DEV = 128
TOKENS = 1024
SEQS = 32
N_CTX = 8


def draw_queries(key, part):
    key = jax.random.fold_in(key, 11)
    width = HEADS * HEAD_DIM
    base_values = jnp.clip(jax.random.normal(key, (SEQS, TOKENS, width)), -5.0, 5.0)
    return base_values.astype(jnp.bfloat16)


def draw_key_vectors(key, part):
    key = jax.random.fold_in(key, 17)
    width = KV_HEADS * HEAD_DIM
    base_values = jnp.clip(jax.random.normal(key, (SEQS, TOKENS, width)), -5.0, 5.0)
    return base_values.astype(jnp.bfloat16)


def block_shuffle(perm_key):
    return jax.random.permutation(perm_key, BPD)


def sequence_plan(row_key):
    row_keys = jax.random.split(row_key, 4)
    shard_order = jax.random.permutation(row_keys[0], N_CTX)
    offsets = jax.random.permutation(row_keys[1], N_CTX)
    inverse = jnp.argsort(shard_order)
    orders = jax.vmap(block_shuffle)(jax.random.split(row_keys[2], N_CTX))
    shuffles = jax.vmap(block_shuffle)(jax.random.split(row_keys[3], N_CTX))
    destination = jnp.arange(N_CTX)[:, None]
    turn_index = jnp.arange(BPD)[None, :]
    source = inverse[(destination - offsets[turn_index % N_CTX]) % N_CTX]
    block_ids = source * BPD + orders[source, turn_index]
    placed = jnp.take_along_axis(block_ids, shuffles, axis=1)
    return placed.reshape(-1).astype(jnp.int32)


def draw_shard_plan(key, part):
    key = jax.random.fold_in(key, 23)
    return jax.vmap(sequence_plan)(jax.random.split(key, SEQS))


def with_ends(result, stream_key, low, high):
    longest = result.shape.index(max(result.shape))
    spots = []
    for shift in (0, 1):
        where = [jax.random.randint(jax.random.fold_in(stream_key, axis), (), 0, length) for axis, length in enumerate(result.shape)]
        where[longest] = (where[longest] + shift) % result.shape[longest]
        spots.append(tuple(where))
    return result.at[spots[0]].set(low).at[spots[1]].set(high)


def raised(array, stream_key, source, target, blocks, factor):
    owner, partner = [(jnp.arange(array.shape[axis_at]) // (array.shape[axis_at] // blocks)).reshape([-1 if axis == axis_at else 1 for axis in range(array.ndim)]) for axis_at in (source, target)]
    chosen = jax.random.permutation(stream_key, blocks)[partner]
    strong = (owner == chosen) | (owner == (partner + blocks // 2) % blocks)
    return jnp.where(strong, factor * array, array)


def steps_of(key, shape, pieces, least, high):
    gain, own = 1.0, jax.random.fold_in(key, 6)
    for axis_at, blocks in pieces:
        heights = jnp.exp(jax.random.uniform(jax.random.fold_in(own, axis_at), (blocks,), jnp.float32, least / len(pieces), high / len(pieces)))
        gain = gain * jnp.repeat(heights, shape[axis_at] // blocks).reshape([-1 if axis == axis_at else 1 for axis in range(len(shape))])
    return gain


def length_profile(amount, total, limit, skew):
    portions = [(1 << 20) // math.isqrt(grade ** skew) + 1 for grade in range(2, amount + 1)]
    surplus, counts = total - limit - (amount - 1), [1] * (amount - 1)
    while surplus > 0:
        movable = [i for i in range(amount - 1) if counts[i] < limit]
        pool, budget = sum([portions[i] for i in movable]), surplus
        for i in movable:
            extra = min(limit - counts[i], max(1, budget * portions[i] // pool), surplus)
            counts[i] = counts[i] + extra
            surplus = surplus - extra
    return np.array([limit] + counts)


def uneven_parts(rng, number_of, total, most, lean):
    if number_of == 2:
        one = jax.random.randint(rng, (), max(1, total - most), min(most, total - 1) + 1)
        return jnp.stack([one, total - one])
    sizes = jnp.asarray(length_profile(number_of, total, most, lean), jnp.int32)
    twos = (number_of - 1) // 2
    giver, sink = sizes[1:1 + 2 * twos:2], sizes[2:2 + 2 * twos:2]
    margin = jnp.minimum(giver - 1, most - sink)
    moved = jax.random.randint(jax.random.fold_in(rng, 1), (twos,), 0, 1 << 20) % (margin + 1)
    sizes = sizes.at[1:1 + 2 * twos:2].set(giver - moved).at[2:2 + 2 * twos:2].set(sink + moved)
    return sizes[jax.random.permutation(jax.random.fold_in(rng, 2), number_of)]


def gaussian(key, shape, spread, bound, pieces=(), kind=jnp.bfloat16):
    result = spread * jax.random.normal(key, shape, jnp.float32)
    if pieces:
        result = result * steps_of(key, shape, pieces, -0.22, 0.18)
    return jnp.clip(result, -bound, bound).astype(kind)


def gaussian_with(rng, extent, scale, reach, cuts, heavy, kind=jnp.bfloat16):
    drawn = scale * jax.random.normal(rng, extent, jnp.float32)
    if cuts:
        drawn = drawn * steps_of(rng, extent, cuts, -0.22, 0.18)
    return jnp.clip(raised(drawn, jax.random.fold_in(rng, 3), *heavy), -reach, reach).astype(kind)


def setup_inputs(seed: int = 0) -> dict:
    keys = jax.random.split(jax.random.key(seed), 9)
    return {
        "queries": draw_queries(jax.random.fold_in(keys[8], 71), 0),
        "key_vectors": draw_key_vectors(jax.random.fold_in(keys[8], 71), 0),
        "activations": gaussian_with(keys[2], (SEQS, TOKENS, D), 1.0, 6.0, ((0, 32), (1, 8)), (1, 2, 8, 2.0)),
        "value_weight": gaussian(keys[3], (D, KV_HEADS * HEAD_DIM), D ** -0.5, 0.09375, ((0, 256),)),
        "attended_grad": gaussian(keys[4], (SEQS, TOKENS, HEADS * HEAD_DIM), 1.0, 6.0, ((0, 32), (1, 8))),
        "doc_ids": jax.vmap(lambda own: jnp.searchsorted(jnp.cumsum(uneven_parts(own, 2 * N_CTX, TOKENS, TOKENS // 2, 2)), jnp.arange(TOKENS), side="right"))(jax.random.split(keys[5], SEQS)).reshape((SEQS, TOKENS)).astype(jnp.int32),
        "shard_plan": draw_shard_plan(jax.random.fold_in(keys[8], 71), 0),
        "round_bits": with_ends(jax.random.randint(keys[7], (N_CTX, TOKENS, 2 * KV_HEADS), 0, 1073741824), jax.random.fold_in(keys[7], 1), 0, 1073741823).astype(jnp.int32),
    }


def reference(queries, key_vectors, activations, value_weight, attended_grad, doc_ids, shard_plan, round_bits):
    group_size = HEADS // KV_HEADS
    block_rows = TOK_DEV // BPD
    scale_factor = HEAD_DIM ** -0.5
    kv_width = KV_HEADS * HEAD_DIM
    places = jnp.arange(TOKENS, dtype=jnp.int32)

    def one_sequence(weight_sum, inputs):
        query_rows, key_rows, act_rows, grad_rows, doc_row, plan_row = inputs
        place_pos = (jnp.take(plan_row, places // block_rows) * block_rows + places % block_rows).astype(jnp.int32)
        inverse = jnp.argsort(place_pos).astype(jnp.int32)
        place_doc = jnp.take(doc_row, place_pos)
        query_bal = jnp.take(query_rows, place_pos, axis=0)
        key_bal = jnp.take(key_rows, place_pos, axis=0)
        act_bal = jnp.take(act_rows, place_pos, axis=0)
        grad_bal = jnp.take(grad_rows, place_pos, axis=0)
        value_bal = jnp.dot(act_bal, value_weight, preferred_element_type=jnp.float32).astype(jnp.bfloat16)
        allowed = (place_doc[:, None] == place_doc[None, :]) & (place_pos[None, :] <= place_pos[:, None])
        query_groups = query_bal.reshape(TOKENS, KV_HEADS, group_size, HEAD_DIM).transpose(1, 0, 2, 3)
        grad_groups = grad_bal.reshape(TOKENS, KV_HEADS, group_size, HEAD_DIM).transpose(1, 0, 2, 3)
        key_groups = key_bal.reshape(TOKENS, KV_HEADS, HEAD_DIM).transpose(1, 0, 2)
        value_groups = value_bal.reshape(TOKENS, KV_HEADS, HEAD_DIM).transpose(1, 0, 2)

        def one_group(group_inputs):
            query_part, key_part, value_part, grad_part = group_inputs
            query_wide = query_part.astype(jnp.float32)
            key_wide = key_part.astype(jnp.float32)
            value_wide = value_part.astype(jnp.float32)
            grad_wide = grad_part.astype(jnp.float32)
            scores = jnp.einsum('igd,jd->gij', query_wide, key_wide) * scale_factor
            masked = jnp.where(allowed, scores, -jnp.inf)
            row_top = jnp.max(masked, axis=-1)
            weights = jnp.exp(masked - row_top[..., None])
            row_sum = jnp.sum(weights, axis=-1)
            weights_low = lax.optimization_barrier(weights.astype(jnp.bfloat16)).astype(jnp.float32)
            attended_part = (jnp.einsum('gij,jd->gid', weights_low, value_wide) / row_sum[..., None]).astype(jnp.bfloat16)
            log_total = row_top + jnp.log(row_sum)
            row_delta = jnp.sum(grad_wide.transpose(1, 0, 2) * attended_part.astype(jnp.float32), axis=-1)
            probability = jnp.where(allowed, jnp.exp(scores - log_total[..., None]), 0.0)
            prob_low = lax.optimization_barrier(probability.astype(jnp.bfloat16)).astype(jnp.float32)
            prob_grad = jnp.einsum('igd,jd->gij', grad_wide, value_wide)
            score_grad = lax.optimization_barrier((probability * (prob_grad - row_delta[..., None])).astype(jnp.bfloat16)).astype(jnp.float32)
            query_grad_part = (jnp.einsum('gij,jd->igd', score_grad, key_wide) * scale_factor).astype(jnp.bfloat16)
            score_blocks = score_grad.reshape(group_size, N_CTX, TOK_DEV, TOKENS)
            prob_blocks = prob_low.reshape(group_size, N_CTX, TOK_DEV, TOKENS)
            query_blocks = query_wide.reshape(N_CTX, TOK_DEV, group_size, HEAD_DIM)
            grad_blocks = grad_wide.reshape(N_CTX, TOK_DEV, group_size, HEAD_DIM)
            key_terms = jnp.einsum('gctj,ctgd->cjd', score_blocks, query_blocks) * scale_factor
            value_terms = jnp.einsum('gctj,ctgd->cjd', prob_blocks, grad_blocks)
            return attended_part, query_grad_part, key_terms, value_terms

        attended_groups, query_grad_groups, key_terms, value_terms = lax.map(one_group, (query_groups, key_groups, value_groups, grad_groups))
        attended_bal = attended_groups.transpose(2, 0, 1, 3).reshape(TOKENS, HEADS * HEAD_DIM)
        query_grad_bal = query_grad_groups.transpose(1, 0, 2, 3).reshape(TOKENS, HEADS * HEAD_DIM)
        terms = jnp.stack([key_terms, value_terms], axis=0).reshape(2, KV_HEADS, N_CTX, N_CTX, TOK_DEV, HEAD_DIM)
        owners = jnp.arange(N_CTX, dtype=jnp.int32)
        running = jnp.zeros((2, KV_HEADS, N_CTX, TOK_DEV, HEAD_DIM), jnp.bfloat16)
        for turn_index in range(N_CTX):
            contributors = (owners + turn_index) % N_CTX
            partial_value = terms[:, :, contributors, owners]
            bits_now = round_bits[turn_index].reshape(N_CTX, TOK_DEV, 2, KV_HEADS).transpose(2, 3, 0, 1)
            jitter = bits_now.astype(jnp.float32) * (2.0 ** -30) - 0.5
            summed = running.astype(jnp.float32) + partial_value
            running = (summed + jitter[..., None] * jnp.abs(summed) * (2.0 ** -4)).astype(jnp.bfloat16)
        key_grad_bal = running[0].transpose(1, 2, 0, 3).reshape(TOKENS, kv_width)
        value_grad_bal = running[1].transpose(1, 2, 0, 3).reshape(TOKENS, kv_width)
        weight_part = jnp.dot(act_bal.T, value_grad_bal, preferred_element_type=jnp.float32)
        outputs = (jnp.take(attended_bal, inverse, axis=0), jnp.take(query_grad_bal, inverse, axis=0), jnp.take(key_grad_bal, inverse, axis=0))
        return weight_sum + weight_part, outputs

    start_sum = jnp.zeros((D, kv_width), jnp.float32)
    weight_grad, stacked = lax.scan(one_sequence, start_sum, (queries, key_vectors, activations, attended_grad, doc_ids, shard_plan))
    return stacked[0], stacked[1], stacked[2], weight_grad
```

```python
import functools

import jax
import jax.numpy as jnp
from jax import lax
from jax.experimental import pallas as pl
from jax.experimental.pallas import tpu as pltpu
from jax.sharding import PartitionSpec as P

MESH = pl.DeviceIdType.MESH
ANY = pl.BlockSpec(memory_space=pl.ANY)
BF = jnp.bfloat16
F32 = jnp.float32
I32 = jnp.int32

N_CTX = 8
N_Z = 8
HEAD = 128
GROUP = 8
TOK = 128
HALF = 64
SEQ = 1024
BLOCK = 32
BAND = 512
WIN = BAND + BLOCK
D = 4096
KVW = 512
COLS = 256
PAD_ROWS = SEQ + BAND + 128
SCALE = HEAD**-0.5
LOG2E = 1.4426950408889634
NEG = -1e30


def vmem(shape, dtype):
    return pltpu.VMEM(shape, dtype)


def dma(*shape):
    return pltpu.SemaphoreType.DMA(shape)


class Place:
    def __init__(self):
        self.dp = lax.axis_index("dp")
        self.ctx = lax.axis_index("ctx")
        self.core = self.dp % 2
        self.z = (self.dp // 2) % N_Z
        self.ylo = self.dp // 16
        self.base = self.dp - self.core
        self.par = self.ctx // 4
        self.head = self.ctx % 4
        self.partner = (self.base + 1 - self.core, self.ctx)
        self.across = (self.dp + 16 - 32 * self.ylo, self.ctx)
        self.up = (self.ylo * 16 + (self.z + 1) % N_Z * 2 + self.core, self.ctx)
        self.down = (self.ylo * 16 + (self.z + N_Z - 1) % N_Z * 2 + self.core, self.ctx)

    def is_me(self, core, ctx):
        return (self.core == core) & (self.ctx == ctx)


def greet(me):
    barrier = pltpu.get_barrier_semaphore()
    for core in range(2):
        for ctx in range(N_CTX):

            @pl.when(jnp.logical_not(me.is_me(core, ctx)))
            def _(core=core, ctx=ctx):
                pl.semaphore_signal(barrier, inc=1, device_id=(me.base + core, jnp.int32(ctx)), device_id_type=MESH)

    for other in (me.across, me.up, me.down):
        pl.semaphore_signal(barrier, inc=1, device_id=other, device_id_type=MESH)
    pl.semaphore_wait(barrier, 2 * N_CTX + 2)


def remote(src, dst, ssem, rsem, device):
    return pltpu.make_async_remote_copy(
        src_ref=src, dst_ref=dst, send_sem=ssem, recv_sem=rsem, device_id=device, device_id_type=MESH
    )


def push(me, src, dst, ssem, rsem, core, ctx):
    mine = me.is_me(core, ctx)

    @pl.when(mine)
    def _():
        pltpu.make_async_copy(src, dst, rsem).start()

    @pl.when(jnp.logical_not(mine))
    def _():
        remote(src, dst, ssem, rsem, (me.base + core, jnp.int32(ctx))).start()


def pushed(me, src, ssem, core, ctx):
    @pl.when(jnp.logical_not(me.is_me(core, ctx)))
    def _():
        remote(src, src, ssem, ssem, (me.base + core, jnp.int32(ctx))).wait_send()


def landed(dst, rsem):
    pltpu.make_async_copy(dst, dst, rsem).wait()


def in_kernel(
    q, g, k, x, w, lens, plc, qa, ga, ka, va, lensp, plcp,
    wfull, xv, vbuf, vacc,
    w_s, w_r, q_s, q_r, g_s, g_r, k_s, k_r, v_s, v_r, one_s, one_r, up_s, up_r, dn_s, dn_r, loc,
):
    me = Place()
    greet(me)
    plane = [(core, ctx) for core in range(2) for ctx in range(N_CTX)]

    def w_src(core):
        return w.at[:, pl.ds(core * COLS, COLS)]

    row = pl.multiple_of(me.core * 128 + me.ctx * 16, 16)
    w_dst = wfull.at[me.ylo, me.z, pl.ds(row, 16), :]
    for n, (core, ctx) in enumerate(plane):
        push(me, w_src(core), w_dst, w_s.at[n], w_r.at[me.core * N_CTX + me.ctx], core, ctx)

    own_x = pltpu.make_async_copy(x, xv.at[me.core], loc.at[0])
    own_l = pltpu.make_async_copy(lens, lensp.at[me.core], loc.at[1])
    own_p = pltpu.make_async_copy(plc, plcp.at[me.core], loc.at[2])
    far_x = remote(x, xv.at[me.core], one_s.at[0], one_r.at[0], me.partner)
    far_l = remote(lens, lensp.at[me.core], one_s.at[1], one_r.at[1], me.partner)
    far_p = remote(plc, plcp.at[me.core], one_s.at[2], one_r.at[2], me.partner)
    for copy in (own_x, far_x, own_l, far_l, own_p, far_p):
        copy.start()

    def k_src(j):
        return k.at[:, pl.ds(j * HEAD, HEAD)]

    def wide(ref, core, j):
        return ref.at[pl.ds(core * HALF, HALF), pl.ds(j * GROUP * HEAD, GROUP * HEAD)]

    spot = pl.multiple_of(me.ctx * TOK, TOK)
    half_spot = pl.multiple_of(me.ctx * HALF, HALF)

    for n in range(8):
        core, j = n // 4, n % 4
        push(me, k_src(j), ka.at[pl.ds(spot, TOK), :], k_s.at[n], k_r.at[me.ctx], core, me.core * 4 + j)
    for n in range(8):
        core, j = n // 4, n % 4
        push(me, wide(q, core, j), qa.at[pl.ds(half_spot, HALF), :], q_s.at[n], q_r.at[me.ctx], core, me.core * 4 + j)
    for n in range(8):
        core, j = n // 4, n % 4
        push(me, wide(g, core, j), ga.at[pl.ds(half_spot, HALF), :], g_s.at[n], g_r.at[me.ctx], core, me.core * 4 + j)

    for n in range(16):
        landed(wfull.at[me.ylo, me.z, pl.ds(n * 16, 16), :], w_r.at[n])
    mine = wfull.at[me.ylo, me.z]
    over = remote(mine, mine, one_s.at[3], one_r.at[3], me.across)
    over.start()
    own_x.wait()
    far_x.wait()
    vacc[...] = jnp.zeros_like(vacc)
    over.wait()

    def project(z):
        for ylo in range(2):
            col = pl.multiple_of(ylo * 2048 + z * 256, 256)
            part = xv[:, :, pl.ds(col, 256)].reshape(2 * TOK, 256)
            vacc[...] += jnp.dot(part, wfull[ylo, z], preferred_element_type=F32)

    def chunk(z):
        return wfull.at[:, z]

    for s in range(4):
        z_up = (me.z + N_Z - s) % N_Z
        up = remote(chunk(z_up), chunk(z_up), up_s.at[s], up_r.at[s], me.up)
        up.start()
        if s < 3:
            z_dn = (me.z + s) % N_Z
            dn = remote(chunk(z_dn), chunk(z_dn), dn_s.at[s], dn_r.at[s], me.down)
            dn.start()
        project(z_up)
        if s > 0:
            project((me.z + s) % N_Z)
        up.wait()
        if s < 3:
            dn.wait()
    project((me.z + N_Z - 4) % N_Z)

    vbuf[...] = vacc[...].astype(BF)

    def v_src(par, jj):
        return vbuf.at[pl.ds(par * TOK, TOK), pl.ds(jj * HEAD, HEAD)]

    routes = [(core, par, jj) for core in range(2) for par in range(2) for jj in range(2)]
    for n, (core, par, jj) in enumerate(routes):
        push(
            me, v_src(par, jj), va.at[pl.ds(spot, TOK), :], v_s.at[n], v_r.at[me.ctx], core,
            par * 4 + me.core * 2 + jj,
        )

    for n, (core, ctx) in enumerate(plane):
        pushed(me, w_src(core), w_s.at[n], core, ctx)
    for n in range(8):
        core, j = n // 4, n % 4
        pushed(me, k_src(j), k_s.at[n], core, me.core * 4 + j)
        pushed(me, wide(q, core, j), q_s.at[n], core, me.core * 4 + j)
        pushed(me, wide(g, core, j), g_s.at[n], core, me.core * 4 + j)
    for n, (core, par, jj) in enumerate(routes):
        pushed(me, v_src(par, jj), v_s.at[n], core, par * 4 + me.core * 2 + jj)
    for copy in (own_l, far_l, own_p, far_p):
        copy.wait()
    for i in range(N_CTX):
        landed(ka.at[pl.ds(i * TOK, TOK), :], k_r.at[i])
        landed(qa.at[pl.ds(i * HALF, HALF), :], q_r.at[i])
        landed(ga.at[pl.ds(i * HALF, HALF), :], g_r.at[i])
        landed(va.at[pl.ds(i * TOK, TOK), :], v_r.at[i])


def exchange_in(q, g, k, x, w, lens, plc):
    return pl.pallas_call(
        in_kernel,
        out_shape=[
            jax.ShapeDtypeStruct((SEQ // 2, GROUP * HEAD), BF),
            jax.ShapeDtypeStruct((SEQ // 2, GROUP * HEAD), BF),
            jax.ShapeDtypeStruct((SEQ, HEAD), BF),
            jax.ShapeDtypeStruct((SEQ, HEAD), BF),
            jax.ShapeDtypeStruct((2,) + lens.shape, I32),
            jax.ShapeDtypeStruct((2,) + plc.shape, I32),
        ],
        in_specs=[ANY] * 7,
        out_specs=[ANY] * 6,
        scratch_shapes=[
            vmem((2, N_Z, 256, COLS), BF), vmem((2, TOK, D), BF), vmem((2 * TOK, COLS), BF), vmem((2 * TOK, COLS), F32),
            dma(16), dma(16), dma(8), dma(8), dma(8), dma(8), dma(8), dma(8), dma(8), dma(8),
            dma(4), dma(4), dma(4), dma(4), dma(3), dma(3), dma(3),
        ],
        compiler_params=pltpu.CompilerParams(
            collective_id=0, has_side_effects=True, vmem_limit_bytes=24 * 2**20
        ),
        cost_estimate=pl.CostEstimate(flops=2 * 256 * D * COLS, bytes_accessed=16 * 2**20, transcendentals=0),
        name="exchange_in",
    )(q, g, k, x, w, lens, plc)


NT = (((1,), (1,)), ((), ()))
TN = (((0,), (0,)), ((), ()))


def attention_kernel(
    plc, q, g, k, v, lens, bits, o, dq, terms, dith,
    kpad, vpad, kt, vt, kacc, vacc,
):
    me = Place()
    step = pl.program_id(0)
    core, par = me.core, me.par

    @pl.when(step == 0)
    def _():
        for pad, src in ((kpad, k), (vpad, v)):
            pad[0:BAND, :] = jnp.zeros((BAND, HEAD), BF)
            pad[BAND : BAND + SEQ, :] = src[...]
            pad[BAND + SEQ :, :] = jnp.zeros((PAD_ROWS - BAND - SEQ, HEAD), BF)
        for b in range(2):
            off = core * HALF + b * BLOCK
            for n in range(12):
                rows = pl.ds(pl.multiple_of(off + n * 128, BLOCK), 128)
                kt[b, :, n * 128 : n * 128 + 128] = kpad[rows, :].T
                vt[b, :, n * 128 : n * 128 + 128] = vpad[rows, :].T

        @pl.loop(0, N_CTX)
        def _(c):
            kacc[c] = jnp.zeros((BAND + SEQ, HEAD), F32)
            vacc[c] = jnp.zeros((BAND + SEQ, HEAD), F32)

    key_row = lax.broadcasted_iota(I32, (WIN, GROUP * BLOCK), 0)
    lane = lax.broadcasted_iota(I32, (1, GROUP * BLOCK), 1) % BLOCK
    for b in range(2):
        block = step * 4 + core * 2 + b
        owner = plc[par, 0, block] // 4
        start = pl.multiple_of(block * BLOCK, BLOCK)
        rows = pl.ds(start, WIN)
        window = pl.ds(pl.multiple_of(step * TOK, TOK), WIN)

        def stacked(ref):
            return jnp.concatenate(
                [ref[b * BLOCK : (b + 1) * BLOCK, h * HEAD : (h + 1) * HEAD] for h in range(GROUP)], axis=0
            )

        def unstack(ref, value):
            for h in range(GROUP):
                ref[b * BLOCK : (b + 1) * BLOCK, h * HEAD : (h + 1) * HEAD] = value[h * BLOCK : (h + 1) * BLOCK]

        qs, gs = stacked(q), stacked(g)
        kw, vw = kpad[rows, :], vpad[rows, :]
        first = lane + BAND - lens[par, pl.ds(block, 1), :]
        allowed = (key_row >= first) & (key_row <= lane + BAND)
        s = lax.dot_general(kw, qs, NT, preferred_element_type=F32) * (SCALE * LOG2E)
        s = jnp.where(allowed, s, NEG)
        top = jnp.max(s, axis=0, keepdims=True)
        weight = jnp.exp2(s - top)
        prob = weight * (1.0 / jnp.sum(weight, axis=0, keepdims=True))
        low = prob.astype(BF)
        out_t = jnp.dot(vt[b, :, window], low, preferred_element_type=F32)
        out = out_t.T.astype(BF)
        unstack(o, out)
        gt = gs.astype(F32).T
        delta = jnp.sum(gt * out_t.astype(BF).astype(F32), axis=0, keepdims=True)
        dprob = lax.dot_general(vw, gs, NT, preferred_element_type=F32)
        dscore = (prob * (dprob - delta)).astype(BF)
        dq_t = jnp.dot(kt[b, :, window], dscore, preferred_element_type=F32)
        unstack(dq, (dq_t * SCALE).T.astype(BF))
        kacc[owner, rows, :] += jnp.dot(dscore, qs, preferred_element_type=F32)
        vacc[owner, rows, :] += jnp.dot(low, gs, preferred_element_type=F32)

    @pl.when(step == N_CTX - 1)
    def _():
        for half in range(2):

            @pl.loop(0, 16)
            def _(n):
                own = plc[par, 0, half * 16 + n] // 4
                src = pl.ds(pl.multiple_of(BAND + (half * 16 + n) * BLOCK, BLOCK), BLOCK)
                dst = pl.ds(pl.multiple_of(n * BLOCK, BLOCK), BLOCK)
                for t in range(N_CTX):
                    c = (own + t) % N_CTX
                    terms[half, 0, t, dst, :] = (kacc[c, src, :] * SCALE).astype(BF)
                    terms[half, 1, t, dst, :] = vacc[c, src, :].astype(BF)

        wanted = [bits[pl.ds(t * 8 + me.head, 1), :] for t in range(N_CTX)]
        wanted += [bits[pl.ds(t * 8 + 4 + me.head, 1), :] for t in range(N_CTX)]
        jitter = jnp.concatenate(wanted, axis=0).astype(F32) * 2.0**-30 - 0.5
        jitter = jnp.concatenate([jitter * 2.0**-4, jnp.zeros((112, SEQ), F32)], axis=0)
        kacc[0, 0:SEQ, :] = jitter.T

        @pl.loop(0, 16)
        def _(n):
            place = plc[par, 0, core * 16 + n]
            dst = pl.ds(pl.multiple_of(n * BLOCK, BLOCK), BLOCK)
            dith[dst, :] = kacc[0, pl.ds(pl.multiple_of(place * BLOCK, BLOCK), BLOCK), :]


def attend(plc, q, g, k, v, lens, bits):
    tile = pl.BlockSpec((HALF, GROUP * HEAD), lambda i, *_: (i, 0))

    def whole(shape):
        return pl.BlockSpec(shape, lambda i, *_: (0,) * len(shape))

    return pl.pallas_call(
        attention_kernel,
        grid_spec=pltpu.PrefetchScalarGridSpec(
            num_scalar_prefetch=1,
            grid=(N_CTX,),
            in_specs=[tile, tile, whole(k.shape), whole(v.shape), whole(lens.shape), whole(bits.shape)],
            out_specs=[tile, tile, whole((2, 2, N_CTX, SEQ // 2, HEAD)), whole((SEQ // 2, HEAD))],
            scratch_shapes=[
                vmem((PAD_ROWS, HEAD), BF), vmem((PAD_ROWS, HEAD), BF),
                vmem((2, HEAD, 1536), BF), vmem((2, HEAD, 1536), BF),
                vmem((N_CTX, BAND + SEQ, HEAD), F32), vmem((N_CTX, BAND + SEQ, HEAD), F32),
            ],
        ),
        out_shape=[
            jax.ShapeDtypeStruct((SEQ // 2, GROUP * HEAD), BF),
            jax.ShapeDtypeStruct((SEQ // 2, GROUP * HEAD), BF),
            jax.ShapeDtypeStruct((2, 2, N_CTX, SEQ // 2, HEAD), BF),
            jax.ShapeDtypeStruct((SEQ // 2, HEAD), F32),
        ],
        compiler_params=pltpu.CompilerParams(vmem_limit_bytes=50 * 2**20),
        cost_estimate=pl.CostEstimate(
            flops=12 * 16 * 256 * WIN * HEAD, bytes_accessed=12 * 2**20, transcendentals=16 * 256 * WIN
        ),
        name="attention",
    )(plc, q, g, k, v, lens, bits)


def out_kernel(
    oc, dqc, terms, dith, x, att, dqo, dko, wg,
    xv, own, part, dv_pair, kd, vd, jit, up_b, dn_b, up_in, dn_in, y_b, y_in, c_b, c_in, wsum,
    o_s, o_r, d_s, d_r, dk_s, dk_r, dv_s, dv_r, one_s, one_r, up_s, up_r, dn_s, dn_r, c_s, c_r, loc,
):
    me = Place()
    greet(me)
    away = 1 - me.core
    swap = remote(terms.at[away], part, one_s.at[0], one_r.at[0], me.partner)
    swap.start()
    keep = pltpu.make_async_copy(terms.at[me.core], own, loc.at[0])
    keep.start()
    jit_in = pltpu.make_async_copy(dith, jit, loc.at[1])
    jit_in.start()
    far_x = remote(x, xv.at[me.core], one_s.at[1], one_r.at[1], me.partner)
    far_x.start()
    own_x = pltpu.make_async_copy(x, xv.at[me.core], loc.at[2])
    own_x.start()

    def wide(ref, j):
        return ref.at[pl.ds(pl.multiple_of(me.core * HALF, HALF), HALF), pl.ds(pl.multiple_of(j * GROUP * HEAD, HEAD), GROUP * HEAD)]

    def home(ref, i):
        return ref.at[pl.ds(i * HALF, HALF), :]

    for src, dst, ssem, rsem in ((oc, att, o_s, o_r), (dqc, dqo, d_s, d_r)):
        for i in range(N_CTX):
            push(me, home(src, i), wide(dst, me.head), ssem.at[i], rsem.at[me.core * 4 + me.head], me.par, i)

    swap.wait()
    keep.wait()
    jit_in.wait()

    @pl.loop(0, 16)
    def _(n):
        rows = pl.ds(pl.multiple_of(n * BLOCK, BLOCK), BLOCK)
        noise = jit[rows, :]
        for f, out in ((0, kd), (1, vd)):
            acc = jnp.zeros((BLOCK, HEAD), F32)
            for t in range(N_CTX):
                total = acc + own[f, t, rows, :].astype(F32) + part[f, t, rows, :].astype(F32)
                u = noise[:, f * 8 + t : f * 8 + t + 1]
                acc = (total + u * jnp.abs(total)).astype(BF).astype(F32)
            out[rows, :] = acc.astype(BF)

    def tile(ref, n):
        return ref.at[pl.ds(n * TOK, TOK), :]

    v_core = me.head // 2
    v_col = pl.multiple_of(me.head % 2 * HEAD, HEAD)
    for n in range(4):
        push(
            me, tile(vd, n), dv_pair.at[pl.ds(pl.multiple_of(me.par * TOK, TOK), TOK), pl.ds(v_col, HEAD)],
            dv_s.at[n], dv_r.at[me.par * 2 + me.head % 2], v_core, me.core * 4 + n,
        )
    k_col = pl.multiple_of(me.head * HEAD, HEAD)
    for n in range(4):
        push(
            me, tile(kd, n), dko.at[:, pl.ds(k_col, HEAD)], dk_s.at[n], dk_r.at[me.head], me.par, me.core * 4 + n
        )
    own_x.wait()
    far_x.wait()
    for n in range(4):
        landed(dv_pair.at[pl.ds(n // 2 * TOK, TOK), pl.ds(n % 2 * HEAD, HEAD)], dv_r.at[n])

    def local_sum(z, ylo):
        col = pl.multiple_of(ylo * 2048 + z * 256, 256)
        return lax.dot_general(
            xv[:, :, pl.ds(col, 256)].reshape(2 * TOK, 256), dv_pair[...], TN, preferred_element_type=F32
        )

    for s in range(4):
        z_up = (me.z + 4 - s) % N_Z
        for ylo in range(2):
            total = local_sum(z_up, ylo)
            if s > 0:
                total = total + up_in[s - 1, ylo].astype(F32)
            up_b[s, ylo] = total.astype(BF)
        up = remote(up_b.at[s], up_in.at[s], up_s.at[s], up_r.at[s], me.up)
        up.start()
        if s < 3:
            z_dn = (me.z + N_Z - 3 + s) % N_Z
            for ylo in range(2):
                total = local_sum(z_dn, ylo)
                if s > 0:
                    total = total + dn_in[s - 1, ylo].astype(F32)
                dn_b[s, ylo] = total.astype(BF)
            dn = remote(dn_b.at[s], dn_in.at[s], dn_s.at[s], dn_r.at[s], me.down)
            dn.start()
        if s == 3:
            for ylo in range(2):
                wsum[ylo] = local_sum(me.z, ylo) + dn_in[2, ylo].astype(F32)
        up.wait()
        if s < 3:
            dn.wait()
    for ylo in range(2):
        wsum[ylo] += up_in[3, ylo].astype(F32)

    y_b[...] = wsum[1 - me.ylo].astype(BF)
    over = remote(y_b, y_in, one_s.at[2], one_r.at[2], me.across)
    over.start()
    over.wait()
    c_b[...] = (wsum[me.ylo] + y_in[...].astype(F32)).astype(BF)

    for n in range(16):
        push(
            me, c_b.at[pl.ds(n * 16, 16), :], c_in.at[me.core, me.ctx], c_s.at[n], c_r.at[me.core * N_CTX + me.ctx],
            n // N_CTX, n % N_CTX,
        )
    for n in range(16):
        landed(c_in.at[n // N_CTX, n % N_CTX], c_r.at[n])
    for core in range(2):
        total = c_in[core, 0].astype(F32)
        for i in range(1, N_CTX):
            total = total + c_in[core, i].astype(F32)
        wg[:, core * COLS : (core + 1) * COLS] = total

    for n in range(16):
        pushed(me, c_b.at[pl.ds(n * 16, 16), :], c_s.at[n], n // N_CTX, n % N_CTX)
    for n in range(4):
        pushed(me, tile(vd, n), dv_s.at[n], v_core, me.core * 4 + n)
        pushed(me, tile(kd, n), dk_s.at[n], me.par, me.core * 4 + n)
        landed(dko.at[:, pl.ds(n * HEAD, HEAD)], dk_r.at[n])
    for i in range(N_CTX):
        pushed(me, home(oc, i), o_s.at[i], me.par, i)
        pushed(me, home(dqc, i), d_s.at[i], me.par, i)
    for core in range(2):
        for j in range(4):
            dst = (pl.ds(core * HALF, HALF), pl.ds(j * GROUP * HEAD, GROUP * HEAD))
            landed(att.at[dst], o_r.at[core * 4 + j])
            landed(dqo.at[dst], d_r.at[core * 4 + j])


def exchange_out(oc, dqc, terms, dith, x):
    slab = (2, 256, COLS)
    return pl.pallas_call(
        out_kernel,
        out_shape=[
            jax.ShapeDtypeStruct((TOK, D), BF),
            jax.ShapeDtypeStruct((TOK, D), BF),
            jax.ShapeDtypeStruct((TOK, KVW), BF),
            jax.ShapeDtypeStruct((16, KVW), F32),
        ],
        in_specs=[ANY] * 5,
        out_specs=[ANY] * 3 + [pl.BlockSpec(memory_space=pltpu.VMEM)],
        scratch_shapes=[
            vmem((2, TOK, D), BF), vmem((2, N_CTX, SEQ // 2, HEAD), BF), vmem((2, N_CTX, SEQ // 2, HEAD), BF),
            vmem((2 * TOK, COLS), BF), vmem((SEQ // 2, HEAD), BF), vmem((SEQ // 2, HEAD), BF), vmem((SEQ // 2, HEAD), F32),
            vmem((4,) + slab, BF), vmem((3,) + slab, BF), vmem((4,) + slab, BF), vmem((3,) + slab, BF),
            vmem((256, COLS), BF), vmem((256, COLS), BF), vmem((256, COLS), BF), vmem((2, N_CTX, 16, COLS), BF),
            vmem(slab, F32),
            dma(8), dma(8), dma(8), dma(8), dma(4), dma(4), dma(4), dma(4), dma(3), dma(3),
            dma(4), dma(4), dma(3), dma(3), dma(16), dma(16), dma(3),
        ],
        compiler_params=pltpu.CompilerParams(
            collective_id=1, has_side_effects=True, vmem_limit_bytes=32 * 2**20
        ),
        cost_estimate=pl.CostEstimate(flops=2 * 256 * D * COLS, bytes_accessed=16 * 2**20, transcendentals=0),
        name="exchange_out",
    )(oc, dqc, terms, dith, x)


def local(queries, key_vectors, activations, value_weight, attended_grad, doc_ids, shard_plan, round_bits):
    docs = jnp.arange(16, dtype=I32)
    starts = jnp.sum((doc_ids < docs[:, None]).astype(I32), axis=1)
    first = jnp.sum(jnp.where(doc_ids == docs[:, None], starts[:, None], 0), axis=0)
    earlier = (jnp.arange(SEQ, dtype=I32) - first).reshape(SEQ // BLOCK, BLOCK)
    lens = jnp.tile(earlier, (1, GROUP))
    blocks = jnp.arange(SEQ // BLOCK, dtype=I32)
    match = shard_plan[0][:, None] == jnp.arange(128, dtype=I32)[None, :]
    place = jnp.sum(jnp.where(match, blocks[:, None], 0), axis=0)
    plc = jnp.broadcast_to(place[None, :], (8, 128))
    qa, ga, ka, va, lensp, plcp = exchange_in(
        queries[0], attended_grad[0], key_vectors[0], activations[0], value_weight, lens, plc
    )
    bits = round_bits.transpose(0, 2, 1).reshape(N_CTX * 8, SEQ)
    oc, dqc, terms, dith = attend(plcp, qa, ga, ka, va, lensp, bits)
    att, dqo, dko, wg = exchange_out(oc, dqc, terms, dith, activations[0])
    return att[None], dqo[None], dko[None], wg


def solution(mesh):
    rows = P("dp", "ctx", None)
    every = P(("dp", "ctx"), None)
    return jax.shard_map(
        local,
        mesh=mesh,
        in_specs=(rows, rows, rows, every, rows, P("dp", None), P("dp", None), P()),
        out_specs=(rows, rows, rows, every),
        check_vma=False,
    )
```

```python
import functools

import jax
import jax.numpy as jnp
from jax import lax
from jax.experimental import pallas as pl
from jax.experimental.pallas import tpu as pltpu
from jax.sharding import PartitionSpec as P

MESH = pl.DeviceIdType.MESH
ANY = pl.BlockSpec(memory_space=pl.ANY)
BF = jnp.bfloat16
F32 = jnp.float32
I32 = jnp.int32

N_CTX = 8
N_Z = 8
HEAD = 128
GROUP = 8
TOK = 128
HALF = 64
SEQ = 1024
BLOCK = 32
BAND = 512
WIN = BAND + BLOCK
D = 4096
KVW = 512
COLS = 256
PAD_ROWS = SEQ + BAND + 128
SCALE = HEAD**-0.5
LOG2E = 1.4426950408889634
NEG = -1e30
SUBS = 2
SUB_ROWS = 512 // SUBS
DROWS = 64


def vmem(shape, dtype):
    return pltpu.VMEM(shape, dtype)


def dma(*shape):
    return pltpu.SemaphoreType.DMA(shape)


class Place:
    def __init__(self):
        self.dp = lax.axis_index("dp")
        self.ctx = lax.axis_index("ctx")
        self.core = self.dp % 2
        self.z = (self.dp // 2) % N_Z
        self.ylo = self.dp // 16
        self.base = self.dp - self.core
        self.par = self.ctx // 4
        self.head = self.ctx % 4
        self.partner = (self.base + 1 - self.core, self.ctx)
        self.across = (self.dp + 16 - 32 * self.ylo, self.ctx)
        self.up = (self.ylo * 16 + (self.z + 1) % N_Z * 2 + self.core, self.ctx)
        self.down = (self.ylo * 16 + (self.z + N_Z - 1) % N_Z * 2 + self.core, self.ctx)

    def is_me(self, core, ctx):
        return (self.core == core) & (self.ctx == ctx)


def greet(me):
    barrier = pltpu.get_barrier_semaphore()
    for core in range(2):
        for ctx in range(N_CTX):

            @pl.when(jnp.logical_not(me.is_me(core, ctx)))
            def _(core=core, ctx=ctx):
                pl.semaphore_signal(barrier, inc=1, device_id=(me.base + core, jnp.int32(ctx)), device_id_type=MESH)

    for other in (me.across, me.up, me.down):
        pl.semaphore_signal(barrier, inc=1, device_id=other, device_id_type=MESH)
    pl.semaphore_wait(barrier, 2 * N_CTX + 2)


def remote(src, dst, ssem, rsem, device):
    return pltpu.make_async_remote_copy(
        src_ref=src, dst_ref=dst, send_sem=ssem, recv_sem=rsem, device_id=device, device_id_type=MESH
    )


def push(me, src, dst, ssem, rsem, core, ctx):
    mine = me.is_me(core, ctx)

    @pl.when(mine)
    def _():
        pltpu.make_async_copy(src, dst, rsem).start()

    @pl.when(jnp.logical_not(mine))
    def _():
        remote(src, dst, ssem, rsem, (me.base + core, jnp.int32(ctx))).start()


def pushed(me, src, ssem, core, ctx):
    @pl.when(jnp.logical_not(me.is_me(core, ctx)))
    def _():
        remote(src, src, ssem, ssem, (me.base + core, jnp.int32(ctx))).wait_send()


def landed(dst, rsem):
    pltpu.make_async_copy(dst, dst, rsem).wait()


def in_kernel(
    q, g, k, x, w, lens, plc, qa, ga, ka, va, lensp, plcp,
    wfull, xv, vbuf, vacc,
    w_s, w_r, q_s, q_r, g_s, g_r, k_s, k_r, v_s, v_r, one_s, one_r, up_s, up_r, dn_s, dn_r, loc,
):
    me = Place()
    greet(me)
    plane = [(core, ctx) for core in range(2) for ctx in range(N_CTX)]

    def w_src(core):
        return w.at[:, pl.ds(core * COLS, COLS)]

    row = pl.multiple_of(me.core * 128 + me.ctx * 16, 16)
    w_dst = wfull.at[me.ylo, me.z, pl.ds(row, 16), :]
    for n, (core, ctx) in enumerate(plane):
        push(me, w_src(core), w_dst, w_s.at[n], w_r.at[me.core * N_CTX + me.ctx], core, ctx)

    own_x = pltpu.make_async_copy(x, xv.at[me.core], loc.at[0])
    own_l = pltpu.make_async_copy(lens, lensp.at[me.core], loc.at[1])
    own_p = pltpu.make_async_copy(plc, plcp.at[me.core], loc.at[2])
    far_x = remote(x, xv.at[me.core], one_s.at[0], one_r.at[0], me.partner)
    far_l = remote(lens, lensp.at[me.core], one_s.at[1], one_r.at[1], me.partner)
    far_p = remote(plc, plcp.at[me.core], one_s.at[2], one_r.at[2], me.partner)
    for copy in (own_x, far_x, own_l, far_l, own_p, far_p):
        copy.start()

    def k_src(j):
        return k.at[:, pl.ds(j * HEAD, HEAD)]

    def wide(ref, core, j):
        return ref.at[pl.ds(core * HALF, HALF), pl.ds(j * GROUP * HEAD, GROUP * HEAD)]

    spot = pl.multiple_of(me.ctx * TOK, TOK)
    half_spot = pl.multiple_of(me.ctx * HALF, HALF)

    for n in range(8):
        core, j = n // 4, n % 4
        push(me, k_src(j), ka.at[pl.ds(spot, TOK), :], k_s.at[n], k_r.at[me.ctx], core, me.core * 4 + j)
    for n in range(16):
        landed(wfull.at[me.ylo, me.z, pl.ds(n * 16, 16), :], w_r.at[n])
    mine = wfull.at[me.ylo, me.z]
    over = remote(mine, mine, one_s.at[3], one_r.at[3], me.across)
    over.start()

    def piece(z, sub):
        ylo = me.ylo if sub < SUBS // 2 else 1 - me.ylo
        return wfull.at[ylo, z, pl.ds(sub % (SUBS // 2) * SUB_ROWS, SUB_ROWS), :]

    def ring(s, sub):
        z_up, z_dn = (me.z + N_Z - s) % N_Z, (me.z + s) % N_Z
        n = s * SUBS + sub
        up = remote(piece(z_up, sub), piece(z_up, sub), up_s.at[n], up_r.at[n], me.up)
        dn = remote(piece(z_dn, sub), piece(z_dn, sub), dn_s.at[n], dn_r.at[n], me.down)
        if s < 3:
            return [up, dn]
        return [up] if sub % 2 == 0 else [dn]

    started = {}

    def go(s, sub):
        started[s, sub] = ring(s, sub)
        for copy in started[s, sub]:
            copy.start()

    for sub in range(SUBS // 2):
        go(0, sub)
    for n in range(8):
        core, j = n // 4, n % 4
        push(me, wide(q, core, j), qa.at[pl.ds(half_spot, HALF), :], q_s.at[n], q_r.at[me.ctx], core, me.core * 4 + j)
    for n in range(8):
        core, j = n // 4, n % 4
        push(me, wide(g, core, j), ga.at[pl.ds(half_spot, HALF), :], g_s.at[n], g_r.at[me.ctx], core, me.core * 4 + j)
    own_x.wait()
    far_x.wait()
    vacc[...] = jnp.zeros_like(vacc)
    over.wait()
    for sub in range(SUBS // 2, SUBS):
        go(0, sub)

    def project(z):
        for ylo in range(2):
            col = pl.multiple_of(ylo * 2048 + z * 256, 256)
            part = xv[:, :, pl.ds(col, 256)].reshape(2 * TOK, 256)
            vacc[...] += jnp.dot(part, wfull[ylo, z], preferred_element_type=F32)

    for s in range(1, 4):
        for sub in range(SUBS):
            up, dn = started[s - 1, sub]
            up.wait_recv()
            dn.wait_recv()
            go(s, sub)
        project((me.z + N_Z - s + 1) % N_Z)
        if s > 1:
            project((me.z + s - 1) % N_Z)
    project((me.z + N_Z - 3) % N_Z)
    project((me.z + 3) % N_Z)
    for sub in range(SUBS):
        started[3, sub][0].wait_recv()
    project((me.z + N_Z - 4) % N_Z)

    vbuf[...] = vacc[...].astype(BF)

    def v_src(par, jj):
        return vbuf.at[pl.ds(par * TOK, TOK), pl.ds(jj * HEAD, HEAD)]

    routes = [(core, par, jj) for core in range(2) for par in range(2) for jj in range(2)]
    for n, (core, par, jj) in enumerate(routes):
        push(
            me, v_src(par, jj), va.at[pl.ds(spot, TOK), :], v_s.at[n], v_r.at[me.ctx], core,
            par * 4 + me.core * 2 + jj,
        )

    for copies in started.values():
        for copy in copies:
            copy.wait_send()
    for n, (core, ctx) in enumerate(plane):
        pushed(me, w_src(core), w_s.at[n], core, ctx)
    for n in range(8):
        core, j = n // 4, n % 4
        pushed(me, k_src(j), k_s.at[n], core, me.core * 4 + j)
        pushed(me, wide(q, core, j), q_s.at[n], core, me.core * 4 + j)
        pushed(me, wide(g, core, j), g_s.at[n], core, me.core * 4 + j)
    for n, (core, par, jj) in enumerate(routes):
        pushed(me, v_src(par, jj), v_s.at[n], core, par * 4 + me.core * 2 + jj)
    for copy in (own_l, far_l, own_p, far_p):
        copy.wait()
    for i in range(N_CTX):
        landed(ka.at[pl.ds(i * TOK, TOK), :], k_r.at[i])
        landed(qa.at[pl.ds(i * HALF, HALF), :], q_r.at[i])
        landed(ga.at[pl.ds(i * HALF, HALF), :], g_r.at[i])
        landed(va.at[pl.ds(i * TOK, TOK), :], v_r.at[i])


def exchange_in(q, g, k, x, w, lens, plc):
    return pl.pallas_call(
        in_kernel,
        out_shape=[
            jax.ShapeDtypeStruct((SEQ // 2, GROUP * HEAD), BF),
            jax.ShapeDtypeStruct((SEQ // 2, GROUP * HEAD), BF),
            jax.ShapeDtypeStruct((SEQ, HEAD), BF),
            jax.ShapeDtypeStruct((SEQ, HEAD), BF),
            jax.ShapeDtypeStruct((2,) + lens.shape, I32),
            jax.ShapeDtypeStruct((2,) + plc.shape, I32),
        ],
        in_specs=[ANY] * 7,
        out_specs=[ANY] * 6,
        scratch_shapes=[
            vmem((2, N_Z, 256, COLS), BF), vmem((2, TOK, D), BF), vmem((2 * TOK, COLS), BF), vmem((2 * TOK, COLS), F32),
            dma(16), dma(16), dma(8), dma(8), dma(8), dma(8), dma(8), dma(8), dma(8), dma(8),
            dma(4), dma(4), dma(4 * SUBS), dma(4 * SUBS), dma(4 * SUBS), dma(4 * SUBS), dma(3),
        ],
        compiler_params=pltpu.CompilerParams(
            collective_id=0, has_side_effects=True, vmem_limit_bytes=60 * 2**20
        ),
        cost_estimate=pl.CostEstimate(flops=2 * 256 * D * COLS, bytes_accessed=16 * 2**20, transcendentals=0),
        name="exchange_in",
    )(q, g, k, x, w, lens, plc)


NT = (((1,), (1,)), ((), ()))
TN = (((0,), (0,)), ((), ()))


def attention_kernel(
    plc, q, g, k, v, lens, bits, o, dq, terms, dith,
    kpad, vpad, kt, vt, kacc, vacc,
):
    me = Place()
    step = pl.program_id(0)
    core, par = me.core, me.par

    @pl.when(step == 0)
    def _():
        for pad, src in ((kpad, k), (vpad, v)):
            pad[0:BAND, :] = jnp.zeros((BAND, HEAD), BF)
            pad[BAND : BAND + SEQ, :] = src[...]
            pad[BAND + SEQ :, :] = jnp.zeros((PAD_ROWS - BAND - SEQ, HEAD), BF)
        for b in range(2):
            off = core * HALF + b * BLOCK
            for n in range(12):
                rows = pl.ds(pl.multiple_of(off + n * 128, BLOCK), 128)
                kt[b, :, n * 128 : n * 128 + 128] = kpad[rows, :].T
                vt[b, :, n * 128 : n * 128 + 128] = vpad[rows, :].T

        @pl.loop(0, N_CTX)
        def _(c):
            kacc[c] = jnp.zeros((BAND + SEQ, HEAD), F32)
            vacc[c] = jnp.zeros((BAND + SEQ, HEAD), F32)

    key_row = lax.broadcasted_iota(I32, (WIN, GROUP * BLOCK), 0)
    lane = lax.broadcasted_iota(I32, (1, GROUP * BLOCK), 1) % BLOCK
    for b in range(2):
        block = step * 4 + core * 2 + b
        owner = plc[par, 0, block] // 4
        start = pl.multiple_of(block * BLOCK, BLOCK)
        rows = pl.ds(start, WIN)
        window = pl.ds(pl.multiple_of(step * TOK, TOK), WIN)

        def stacked(ref):
            return jnp.concatenate(
                [ref[b * BLOCK : (b + 1) * BLOCK, h * HEAD : (h + 1) * HEAD] for h in range(GROUP)], axis=0
            )

        def unstack(ref, value):
            for h in range(GROUP):
                ref[b * BLOCK : (b + 1) * BLOCK, h * HEAD : (h + 1) * HEAD] = value[h * BLOCK : (h + 1) * BLOCK]

        qs, gs = stacked(q), stacked(g)
        kw, vw = kpad[rows, :], vpad[rows, :]
        first = lane + BAND - lens[par, pl.ds(block, 1), :]
        allowed = (key_row >= first) & (key_row <= lane + BAND)
        s = lax.dot_general(kw, qs, NT, preferred_element_type=F32) * (SCALE * LOG2E)
        s = jnp.where(allowed, s, NEG)
        top = jnp.max(s, axis=0, keepdims=True)
        weight = jnp.exp2(s - top)
        prob = weight * (1.0 / jnp.sum(weight, axis=0, keepdims=True))
        low = prob.astype(BF)
        out_t = jnp.dot(vt[b, :, window], low, preferred_element_type=F32)
        out = out_t.T.astype(BF)
        unstack(o, out)
        gt = gs.astype(F32).T
        delta = jnp.sum(gt * out_t.astype(BF).astype(F32), axis=0, keepdims=True)
        dprob = lax.dot_general(vw, gs, NT, preferred_element_type=F32)
        dscore = (prob * (dprob - delta)).astype(BF)
        dq_t = jnp.dot(kt[b, :, window], dscore, preferred_element_type=F32)
        unstack(dq, (dq_t * SCALE).T.astype(BF))
        kacc[owner, rows, :] += jnp.dot(dscore, qs, preferred_element_type=F32)
        vacc[owner, rows, :] += jnp.dot(low, gs, preferred_element_type=F32)

    @pl.when(step == N_CTX - 1)
    def _():
        for half in range(2):

            @pl.loop(0, 16)
            def _(n):
                own = plc[par, 0, half * 16 + n] // 4
                src = pl.ds(pl.multiple_of(BAND + (half * 16 + n) * BLOCK, BLOCK), BLOCK)
                dst = pl.ds(pl.multiple_of(n * BLOCK, BLOCK), BLOCK)
                for t in range(N_CTX):
                    c = (own + t) % N_CTX
                    terms[half, 0, t, dst, :] = (kacc[c, src, :] * SCALE).astype(BF)
                    terms[half, 1, t, dst, :] = vacc[c, src, :].astype(BF)

        wanted = [bits[pl.ds(t * 8 + me.head, 1), :] for t in range(N_CTX)]
        wanted += [bits[pl.ds(t * 8 + 4 + me.head, 1), :] for t in range(N_CTX)]
        jitter = jnp.concatenate(wanted, axis=0).astype(F32) * 2.0**-30 - 0.5
        jitter = jnp.concatenate([jitter * 2.0**-4, jnp.zeros((112, SEQ), F32)], axis=0)
        kacc[0, 0:SEQ, :] = jitter.T

        @pl.loop(0, 16)
        def _(n):
            place = plc[par, 0, core * 16 + n]
            dst = pl.ds(pl.multiple_of(n * BLOCK, BLOCK), BLOCK)
            dith[dst, :] = kacc[0, pl.ds(pl.multiple_of(place * BLOCK, BLOCK), BLOCK), :]


def attend(plc, q, g, k, v, lens, bits):
    tile = pl.BlockSpec((HALF, GROUP * HEAD), lambda i, *_: (i, 0))

    def whole(shape):
        return pl.BlockSpec(shape, lambda i, *_: (0,) * len(shape))

    return pl.pallas_call(
        attention_kernel,
        grid_spec=pltpu.PrefetchScalarGridSpec(
            num_scalar_prefetch=1,
            grid=(N_CTX,),
            in_specs=[tile, tile, whole(k.shape), whole(v.shape), whole(lens.shape), whole(bits.shape)],
            out_specs=[tile, tile, whole((2, 2, N_CTX, SEQ // 2, HEAD)), whole((SEQ // 2, HEAD))],
            scratch_shapes=[
                vmem((PAD_ROWS, HEAD), BF), vmem((PAD_ROWS, HEAD), BF),
                vmem((2, HEAD, 1536), BF), vmem((2, HEAD, 1536), BF),
                vmem((N_CTX, BAND + SEQ, HEAD), F32), vmem((N_CTX, BAND + SEQ, HEAD), F32),
            ],
        ),
        out_shape=[
            jax.ShapeDtypeStruct((SEQ // 2, GROUP * HEAD), BF),
            jax.ShapeDtypeStruct((SEQ // 2, GROUP * HEAD), BF),
            jax.ShapeDtypeStruct((2, 2, N_CTX, SEQ // 2, HEAD), BF),
            jax.ShapeDtypeStruct((SEQ // 2, HEAD), F32),
        ],
        compiler_params=pltpu.CompilerParams(vmem_limit_bytes=60 * 2**20),
        cost_estimate=pl.CostEstimate(
            flops=12 * 16 * 256 * WIN * HEAD, bytes_accessed=12 * 2**20, transcendentals=16 * 256 * WIN
        ),
        name="attention",
    )(plc, q, g, k, v, lens, bits)


def out_kernel(
    oc, dqc, terms, dith, x, att, dqo, dko, wg,
    xv, own, part, dv_pair, kd, vd, jit, up_b, dn_b, up_in, dn_in, y_b, y_in, c_b, c_in, wsum,
    sw_s, sw_r, ke_s, o_s, o_r, d_s, d_r, dk_s, dk_r, dv_s, dv_r, one_s, one_r, up_s, up_r, dn_s, dn_r, c_s, c_r, loc,
):
    me = Place()
    greet(me)
    away = 1 - me.core
    def rows_of(n):
        return pl.ds(n * TOK, TOK)

    swaps, keeps = [], []
    for n in range(4):
        src, dst = terms.at[away, :, :, rows_of(n), :], part.at[:, :, rows_of(n), :]
        swaps.append(remote(src, dst, sw_s.at[n], sw_r.at[n], me.partner))
        keeps.append(
            pltpu.make_async_copy(terms.at[me.core, :, :, rows_of(n), :], own.at[:, :, rows_of(n), :], ke_s.at[n])
        )
    jit_in = pltpu.make_async_copy(dith, jit, loc.at[0])
    far_x = remote(x, xv.at[me.core], one_s.at[1], one_r.at[1], me.partner)
    own_x = pltpu.make_async_copy(x, xv.at[me.core], loc.at[1])
    jit_in.start()
    for n in range(4):
        swaps[n].start()
        keeps[n].start()
    far_x.start()
    own_x.start()

    def tile(ref, n):
        return ref.at[rows_of(n), :]

    v_core = me.head // 2
    v_col = pl.multiple_of(me.head % 2 * HEAD, HEAD)
    k_col = pl.multiple_of(me.head * HEAD, HEAD)
    v_dst = dv_pair.at[pl.ds(pl.multiple_of(me.par * TOK, TOK), TOK), pl.ds(v_col, HEAD)]
    k_dst = dko.at[:, pl.ds(k_col, HEAD)]
    jit_in.wait()
    for n in range(4):
        swaps[n].wait_recv()
        keeps[n].wait()

        @pl.loop(0, TOK // DROWS)
        def _(m, n=n):
            rows = pl.ds(pl.multiple_of(n * TOK + m * DROWS, DROWS), DROWS)
            noise = jit[rows, :]
            for f, out in ((0, kd), (1, vd)):
                acc = jnp.zeros((DROWS, HEAD), F32)
                for t in range(N_CTX):
                    total = acc + (own[f, t, rows, :].astype(F32) + part[f, t, rows, :].astype(F32))
                    u = noise[:, f * 8 + t : f * 8 + t + 1]
                    acc = (total + u * jnp.abs(total)).astype(BF).astype(F32)
                out[rows, :] = acc.astype(BF)

        push(me, tile(vd, n), v_dst, dv_s.at[n], dv_r.at[me.par * 2 + me.head % 2], v_core, me.core * 4 + n)
    own_x.wait()
    far_x.wait()
    for n in range(4):
        landed(dv_pair.at[pl.ds(n // 2 * TOK, TOK), pl.ds(n % 2 * HEAD, HEAD)], dv_r.at[n])

    def sub_ylo(sub):
        return 1 - me.ylo if sub == 0 else me.ylo

    def local_sum(z, ylo):
        col = pl.multiple_of(ylo * 2048 + z * 256, 256)
        return lax.dot_general(
            xv[:, :, pl.ds(col, 256)].reshape(2 * TOK, 256), dv_pair[...], TN, preferred_element_type=F32
        )

    ways = ((1, up_b, up_in, up_s, up_r, me.up), (-1, dn_b, dn_in, dn_s, dn_r, me.down))

    def ring(w, s, sub):
        _, buf, inn, ssem, rsem, to = ways[w]
        n = s * 2 + sub
        return remote(buf.at[n], inn.at[n], ssem.at[n], rsem.at[n], to)

    started = {}

    def go(w, s, sub):
        sign, buf, inn = ways[w][:3]
        n = s * 2 + sub
        total = local_sum((me.z + N_Z + sign * (4 - s)) % N_Z, sub_ylo(sub))
        if (w, s - 1, sub) in started:
            started[w, s - 1, sub].wait_recv()
            total = total + inn[n - 2].astype(F32)
        buf[n] = total.astype(BF)
        started[w, s, sub] = ring(w, s, sub)
        started[w, s, sub].start()

    go(0, 0, 0)
    go(1, 0, 1)

    def wide(ref, j):
        cols = pl.ds(pl.multiple_of(j * GROUP * HEAD, HEAD), GROUP * HEAD)
        return ref.at[pl.ds(pl.multiple_of(me.core * HALF, HALF), HALF), cols]

    def home(ref, i):
        return ref.at[pl.ds(i * HALF, HALF), :]

    for src, dst, ssem, rsem in ((oc, att, o_s, o_r), (dqc, dqo, d_s, d_r)):
        for i in range(N_CTX):
            push(me, home(src, i), wide(dst, me.head), ssem.at[i], rsem.at[me.core * 4 + me.head], me.par, i)
    for n in range(4):
        push(me, tile(kd, n), k_dst, dk_s.at[n], dk_r.at[me.head], me.par, me.core * 4 + n)

    for s in range(1, 4):
        for sub in range(2):
            go(0, s, sub)
            go(1, s, sub)

    def finish(sub):
        total = local_sum(me.z, sub_ylo(sub))
        for w in range(2):
            started[w, 3, sub].wait_recv()
            total = total + ways[w][2][6 + sub].astype(F32)
        return total

    y_b[...] = finish(0).astype(BF)
    over = remote(y_b, y_in, one_s.at[2], one_r.at[2], me.across)
    over.start()
    wsum[...] = finish(1)
    over.wait()
    c_b[...] = (wsum[...] + y_in[...].astype(F32)).astype(BF)
    for n in range(16):
        push(
            me, c_b.at[pl.ds(n * 16, 16), :], c_in.at[me.core, me.ctx], c_s.at[n], c_r.at[me.core * N_CTX + me.ctx],
            n // N_CTX, n % N_CTX,
        )
    for n in range(16):
        landed(c_in.at[n // N_CTX, n % N_CTX], c_r.at[n])
    for core in range(2):
        total = c_in[core, 0].astype(F32)
        for i in range(1, N_CTX):
            total = total + c_in[core, i].astype(F32)
        wg[:, core * COLS : (core + 1) * COLS] = total

    for n in range(4):
        swaps[n].wait_send()
    for copy in started.values():
        copy.wait_send()
    for n in range(16):
        pushed(me, c_b.at[pl.ds(n * 16, 16), :], c_s.at[n], n // N_CTX, n % N_CTX)
    for n in range(4):
        pushed(me, tile(vd, n), dv_s.at[n], v_core, me.core * 4 + n)
        pushed(me, tile(kd, n), dk_s.at[n], me.par, me.core * 4 + n)
        landed(dko.at[:, pl.ds(n * HEAD, HEAD)], dk_r.at[n])
    for i in range(N_CTX):
        pushed(me, home(oc, i), o_s.at[i], me.par, i)
        pushed(me, home(dqc, i), d_s.at[i], me.par, i)
    for core in range(2):
        for j in range(4):
            dst = (pl.ds(core * HALF, HALF), pl.ds(j * GROUP * HEAD, GROUP * HEAD))
            landed(att.at[dst], o_r.at[core * 4 + j])
            landed(dqo.at[dst], d_r.at[core * 4 + j])


def exchange_out(oc, dqc, terms, dith, x):
    slab = (256, COLS)
    return pl.pallas_call(
        out_kernel,
        out_shape=[
            jax.ShapeDtypeStruct((TOK, D), BF),
            jax.ShapeDtypeStruct((TOK, D), BF),
            jax.ShapeDtypeStruct((TOK, KVW), BF),
            jax.ShapeDtypeStruct((16, KVW), F32),
        ],
        in_specs=[ANY] * 5,
        out_specs=[ANY] * 3 + [pl.BlockSpec(memory_space=pltpu.VMEM)],
        scratch_shapes=[
            vmem((2, TOK, D), BF), vmem((2, N_CTX, SEQ // 2, HEAD), BF), vmem((2, N_CTX, SEQ // 2, HEAD), BF),
            vmem((2 * TOK, COLS), BF), vmem((SEQ // 2, HEAD), BF), vmem((SEQ // 2, HEAD), BF), vmem((SEQ // 2, HEAD), F32),
            vmem((8,) + slab, BF), vmem((8,) + slab, BF), vmem((8,) + slab, BF), vmem((8,) + slab, BF),
            vmem(slab, BF), vmem(slab, BF), vmem(slab, BF), vmem((2, N_CTX, 16, COLS), BF), vmem(slab, F32),
            dma(4), dma(4), dma(4),
            dma(8), dma(8), dma(8), dma(8), dma(4), dma(4), dma(4), dma(4), dma(3), dma(3),
            dma(8), dma(8), dma(8), dma(8), dma(16), dma(16), dma(2),
        ],
        compiler_params=pltpu.CompilerParams(
            collective_id=1, has_side_effects=True, vmem_limit_bytes=60 * 2**20
        ),
        cost_estimate=pl.CostEstimate(flops=2 * 256 * D * COLS, bytes_accessed=16 * 2**20, transcendentals=0),
        name="exchange_out",
    )(oc, dqc, terms, dith, x)


def local(queries, key_vectors, activations, value_weight, attended_grad, doc_ids, shard_plan, round_bits):
    docs = jnp.arange(16, dtype=I32)
    starts = jnp.sum((doc_ids < docs[:, None]).astype(I32), axis=1)
    first = jnp.sum(jnp.where(doc_ids == docs[:, None], starts[:, None], 0), axis=0)
    earlier = (jnp.arange(SEQ, dtype=I32) - first).reshape(SEQ // BLOCK, BLOCK)
    lens = jnp.tile(earlier, (1, GROUP))
    blocks = jnp.arange(SEQ // BLOCK, dtype=I32)
    match = shard_plan[0][:, None] == jnp.arange(128, dtype=I32)[None, :]
    place = jnp.sum(jnp.where(match, blocks[:, None], 0), axis=0)
    plc = jnp.broadcast_to(place[None, :], (8, 128))
    qa, ga, ka, va, lensp, plcp = exchange_in(
        queries[0], attended_grad[0], key_vectors[0], activations[0], value_weight, lens, plc
    )
    bits = round_bits.transpose(0, 2, 1).reshape(N_CTX * 8, SEQ)
    oc, dqc, terms, dith = attend(plcp, qa, ga, ka, va, lensp, bits)
    att, dqo, dko, wg = exchange_out(oc, dqc, terms, dith, activations[0])
    return att[None], dqo[None], dko[None], wg


def solution(mesh):
    rows = P("dp", "ctx", None)
    every = P(("dp", "ctx"), None)
    return jax.shard_map(
        local,
        mesh=mesh,
        in_specs=(rows, rows, rows, every, rows, P("dp", None), P("dp", None), P()),
        out_specs=(rows, rows, rows, every),
        check_vma=False,
    )
```

```python
import functools

import jax
import jax.numpy as jnp
from jax import lax
from jax.experimental import pallas as pl
from jax.experimental.pallas import tpu as pltpu
from jax.sharding import PartitionSpec as P

MESH = pl.DeviceIdType.MESH
ANY = pl.BlockSpec(memory_space=pl.ANY)
BF = jnp.bfloat16
F32 = jnp.float32
I32 = jnp.int32

N_CTX = 8
N_Z = 8
HEAD = 128
GROUP = 8
TOK = 128
HALF = 64
SEQ = 1024
BLOCK = 32
BAND = 512
WIN = BAND + BLOCK
D = 4096
KVW = 512
COLS = 256
PAD_ROWS = SEQ + BAND + 128
SCALE = HEAD**-0.5
LOG2E = 1.4426950408889634
NEG = -1e30
SUBS = 2
SUB_ROWS = 512 // SUBS
DROWS = 64
EDGE = 3 * BLOCK
SPAN = WIN + 2 * EDGE
CAND = 12

NT = (((1,), (1,)), ((), ()))
TN = (((0,), (0,)), ((), ()))


def vmem(shape, dtype):
    return pltpu.VMEM(shape, dtype)


def dma(*shape):
    return pltpu.SemaphoreType.DMA(shape)


class Place:
    def __init__(self):
        self.dp = lax.axis_index("dp")
        self.ctx = lax.axis_index("ctx")
        self.core = self.dp % 2
        self.z = (self.dp // 2) % N_Z
        self.ylo = self.dp // 16
        self.base = self.dp - self.core
        self.par = self.ctx // 4
        self.head = self.ctx % 4
        self.partner = (self.base + 1 - self.core, self.ctx)
        self.across = (self.dp + 16 - 32 * self.ylo, self.ctx)
        self.up = (self.ylo * 16 + (self.z + 1) % N_Z * 2 + self.core, self.ctx)
        self.down = (self.ylo * 16 + (self.z + N_Z - 1) % N_Z * 2 + self.core, self.ctx)

    def is_me(self, core, ctx):
        return (self.core == core) & (self.ctx == ctx)


def greet(me):
    barrier = pltpu.get_barrier_semaphore()
    for core in range(2):
        for ctx in range(N_CTX):

            @pl.when(jnp.logical_not(me.is_me(core, ctx)))
            def _(core=core, ctx=ctx):
                pl.semaphore_signal(barrier, inc=1, device_id=(me.base + core, jnp.int32(ctx)), device_id_type=MESH)

    for other in (me.across, me.up, me.down):
        pl.semaphore_signal(barrier, inc=1, device_id=other, device_id_type=MESH)
    pl.semaphore_wait(barrier, 2 * N_CTX + 2)


def remote(src, dst, ssem, rsem, device):
    return pltpu.make_async_remote_copy(
        src_ref=src, dst_ref=dst, send_sem=ssem, recv_sem=rsem, device_id=device, device_id_type=MESH
    )


def push(me, src, dst, ssem, rsem, core, ctx):
    mine = me.is_me(core, ctx)

    @pl.when(mine)
    def _():
        pltpu.make_async_copy(src, dst, rsem).start()

    @pl.when(jnp.logical_not(mine))
    def _():
        remote(src, dst, ssem, rsem, (me.base + core, jnp.int32(ctx))).start()


def pushed(me, src, ssem, core, ctx):
    @pl.when(jnp.logical_not(me.is_me(core, ctx)))
    def _():
        remote(src, src, ssem, ssem, (me.base + core, jnp.int32(ctx))).wait_send()


def landed(dst, rsem):
    pltpu.make_async_copy(dst, dst, rsem).wait()


def kernel(
    q, g, k, x, w, lens, plc, tsel, bits, att, dqo, dko, wg,
    wfull, xv, vbuf, vacc, qa, ga, oc, dqc, kpad, vpad, kt, vt, lensv, plcv, bitv, jit,
    tsv, code, pst, kvb, away_t, own_t, part, dv_pair, kd, vd,
    up_b, dn_b, up_in, dn_in, y_b, y_in, c_b, c_in, wsum,
    w_s, w_r, q_s, q_r, g_s, g_r, k_s, k_r, v_s, v_r, one_s, one_r, up_s, up_r, dn_s, dn_r, loc,
    sw_s, sw_r, o_s, o_r, d_s, d_r, dk_s, dk_r, dv_s, dv_r, ru_s, ru_r, rd_s, rd_r, c_s, c_r,
):
    me = Place()
    core, par = me.core, me.par
    for pad in (kpad, vpad):
        pad[0:BAND, :] = jnp.zeros((BAND, HEAD), BF)
        pad[BAND + SEQ :, :] = jnp.zeros((PAD_ROWS - BAND - SEQ, HEAD), BF)
    kvb[:, 0:EDGE, :] = jnp.zeros((16, EDGE, 2 * HEAD), BF)
    kvb[:, EDGE + WIN :, :] = jnp.zeros((16, EDGE, 2 * HEAD), BF)
    down = lax.broadcasted_iota(I32, code.shape, 0)
    right = lax.broadcasted_iota(I32, code.shape, 1)
    code[...] = jnp.where(down % BLOCK == right % BLOCK, down // BLOCK, N_CTX)
    vacc[...] = jnp.zeros_like(vacc)
    greet(me)
    plane = [(n // N_CTX, n % N_CTX) for n in range(2 * N_CTX)]

    def w_src(core):
        return w.at[:, pl.ds(core * COLS, COLS)]

    row = pl.multiple_of(me.core * 128 + me.ctx * 16, 16)
    w_dst = wfull.at[me.ylo, me.z, pl.ds(row, 16), :]
    for n, (to, ctx) in enumerate(plane):
        push(me, w_src(to), w_dst, w_s.at[n], w_r.at[me.core * N_CTX + me.ctx], to, ctx)

    own_x = pltpu.make_async_copy(x, xv.at[me.core], loc.at[0])
    own_l = pltpu.make_async_copy(lens, lensv.at[me.core], loc.at[1])
    own_p = pltpu.make_async_copy(plc, plcv.at[me.core], loc.at[2])
    far_x = remote(x, xv.at[me.core], one_s.at[0], one_r.at[0], me.partner)
    far_l = remote(lens, lensv.at[me.core], one_s.at[1], one_r.at[1], me.partner)
    far_p = remote(plc, plcv.at[me.core], one_s.at[2], one_r.at[2], me.partner)
    own_t_sel = pltpu.make_async_copy(tsel.at[me.core], tsv.at[me.core], loc.at[4])
    far_t_sel = remote(tsel.at[1 - me.core], tsv.at[me.core], one_s.at[4], one_r.at[4], me.partner)
    bits_in = pltpu.make_async_copy(bits, bitv, loc.at[3])
    for copy in (own_x, far_x, own_l, far_l, own_p, far_p, own_t_sel, far_t_sel, bits_in):
        copy.start()

    def k_src(j):
        return k.at[:, pl.ds(j * HEAD, HEAD)]

    def wide(ref, core, j):
        return ref.at[pl.ds(core * HALF, HALF), pl.ds(j * GROUP * HEAD, GROUP * HEAD)]

    spot = pl.multiple_of(BAND + me.ctx * TOK, TOK)
    half_spot = pl.multiple_of(me.ctx * HALF, HALF)

    for n in range(8):
        to, j = n // 4, n % 4
        push(me, k_src(j), kpad.at[pl.ds(spot, TOK), :], k_s.at[n], k_r.at[me.ctx], to, me.core * 4 + j)
    for n in range(16):
        landed(wfull.at[me.ylo, me.z, pl.ds(n * 16, 16), :], w_r.at[n])
    mine = wfull.at[me.ylo, me.z]
    over = remote(mine, mine, one_s.at[3], one_r.at[3], me.across)
    over.start()

    def piece(z, sub):
        ylo = me.ylo if sub < SUBS // 2 else 1 - me.ylo
        return wfull.at[ylo, z, pl.ds(sub % (SUBS // 2) * SUB_ROWS, SUB_ROWS), :]

    def ring(s, sub):
        z_up, z_dn = (me.z + N_Z - s) % N_Z, (me.z + s) % N_Z
        n = s * SUBS + sub
        up = remote(piece(z_up, sub), piece(z_up, sub), up_s.at[n], up_r.at[n], me.up)
        dn = remote(piece(z_dn, sub), piece(z_dn, sub), dn_s.at[n], dn_r.at[n], me.down)
        half = up if sub % 2 == 0 else dn
        return [up, dn] if s < 3 else [half]

    started = {}

    def go(s, sub):
        started[s, sub] = ring(s, sub)
        for copy in started[s, sub]:
            copy.start()

    for sub in range(SUBS // 2):
        go(0, sub)
    for n in range(8):
        to, j = n // 4, n % 4
        push(me, wide(q, to, j), qa.at[pl.ds(half_spot, HALF), :], q_s.at[n], q_r.at[me.ctx], to, me.core * 4 + j)
    for n in range(8):
        to, j = n // 4, n % 4
        push(me, wide(g, to, j), ga.at[pl.ds(half_spot, HALF), :], g_s.at[n], g_r.at[me.ctx], to, me.core * 4 + j)
    own_x.wait()
    far_x.wait()
    over.wait()
    for sub in range(SUBS // 2, SUBS):
        go(0, sub)

    def project(z):
        for ylo in range(2):
            col = pl.multiple_of(ylo * 2048 + z * 256, 256)
            part = xv[:, :, pl.ds(col, 256)].reshape(2 * TOK, 256)
            vacc[...] += jnp.dot(part, wfull[ylo, z], preferred_element_type=F32)

    def transposed(out, pad):
        for b in range(2):
            for n in range(12):
                rows = pl.ds(pl.multiple_of(core * HALF + b * BLOCK + n * 128, BLOCK), 128)
                out[b, :, n * 128 : n * 128 + 128] = pad[rows, :].T

    def stacked(ref, i, b):
        rows = pl.ds(pl.multiple_of(i * HALF + b * BLOCK, BLOCK), BLOCK)
        return jnp.concatenate([ref[rows, h * HEAD : (h + 1) * HEAD] for h in range(GROUP)], axis=0)

    def unstack(ref, i, b, value):
        rows = pl.ds(pl.multiple_of(i * HALF + b * BLOCK, BLOCK), BLOCK)
        for h in range(GROUP):
            ref[rows, h * HEAD : (h + 1) * HEAD] = value[h * BLOCK : (h + 1) * BLOCK]

    def keys_of(i, b):
        block = i * 4 + core * 2 + b
        return block, pl.ds(pl.multiple_of(block * BLOCK, BLOCK), WIN)

    key_row = lax.broadcasted_iota(I32, (WIN, GROUP * BLOCK), 0)
    lane = lax.broadcasted_iota(I32, (1, GROUP * BLOCK), 1) % BLOCK

    def scores(low, high):
        @pl.loop(low, high)
        def _(i):
            landed(qa.at[pl.ds(pl.multiple_of(i * HALF, HALF), HALF), :], q_r.at[i])
            for b in range(2):
                block, rows = keys_of(i, b)
                first = lane + BAND - lensv[par, pl.ds(block, 1), :]
                allowed = (key_row >= first) & (key_row <= lane + BAND)
                s = lax.dot_general(kpad[rows, :], stacked(qa, i, b), NT, preferred_element_type=F32)
                s = jnp.where(allowed, s * (SCALE * LOG2E), NEG)
                weight = jnp.exp2(s - jnp.max(s, axis=0, keepdims=True))
                prob = weight * (1.0 / jnp.sum(weight, axis=0, keepdims=True))
                pst[i * 2 + b] = prob.astype(BF)

    for s in range(1, 4):
        for sub in range(SUBS):
            up, dn = started[s - 1, sub]
            up.wait_recv()
            dn.wait_recv()
            go(s, sub)
        project((me.z + N_Z - s + 1) % N_Z)
        if s > 1:
            project((me.z + s - 1) % N_Z)
    for i in range(N_CTX):
        landed(kpad.at[pl.ds(BAND + i * TOK, TOK), :], k_r.at[i])
    transposed(kt, kpad)
    for copy in (own_l, far_l, own_p, far_p, own_t_sel, far_t_sel):
        copy.wait()
    project((me.z + N_Z - 3) % N_Z)
    project((me.z + 3) % N_Z)
    scores(0, 3)
    for sub in range(SUBS):
        started[3, sub][0].wait_recv()
    project((me.z + N_Z - 4) % N_Z)

    vbuf[...] = vacc[...].astype(BF)

    def v_src(p, jj):
        return vbuf.at[pl.ds(p * TOK, TOK), pl.ds(jj * HEAD, HEAD)]

    routes = [(n // 4, n // 2 % 2, n % 2) for n in range(8)]
    for n, (to, p, jj) in enumerate(routes):
        push(
            me, v_src(p, jj), vpad.at[pl.ds(spot, TOK), :], v_s.at[n], v_r.at[me.ctx], to, p * 4 + me.core * 2 + jj
        )
    scores(3, N_CTX)
    bits_in.wait()
    wanted = [bitv[pl.ds(t * 8 + f * 4 + me.head, 1), :] for f in range(2) for t in range(N_CTX)]
    jitter = (jnp.concatenate(wanted, axis=0).astype(F32) * 2.0**-30 - 0.5) * 2.0**-4
    parts = []
    for _ in range(3):
        parts.append(jitter.astype(BF))
        jitter = jitter - parts[-1].astype(F32)
    at = plcv[par, 0:1, pl.ds(pl.multiple_of(core * (SEQ // 2), SEQ // 2), SEQ // 2)]
    there = lax.broadcasted_iota(I32, (SEQ, SEQ // 2), 0) == at
    moved = jnp.dot(
        jnp.concatenate(parts, axis=0), jnp.where(there, 1.0, 0.0).astype(BF), preferred_element_type=F32
    )
    moved = moved[0:16] + moved[16:32] + moved[32:48]
    jit[...] = jnp.concatenate([moved, jnp.zeros((112, SEQ // 2), F32)], axis=0).T
    for i in range(N_CTX):
        landed(vpad.at[pl.ds(BAND + i * TOK, TOK), :], v_r.at[i])
    transposed(vt, vpad)

    def out_wide(ref, j):
        cols = pl.ds(pl.multiple_of(j * GROUP * HEAD, HEAD), GROUP * HEAD)
        return ref.at[pl.ds(pl.multiple_of(me.core * HALF, HALF), HALF), cols]

    def home(ref, i):
        return ref.at[pl.ds(pl.multiple_of(i * HALF, HALF), HALF), :]

    @pl.loop(0, N_CTX)
    def _(i):
        landed(home(ga, i), g_r.at[i])
        window = pl.ds(pl.multiple_of(i * TOK, TOK), WIN)
        for b in range(2):
            n = i * 2 + b
            _, rows = keys_of(i, b)
            low, qs, gs = pst[n], stacked(qa, i, b), stacked(ga, i, b)
            out_t = jnp.dot(vt[b, :, window], low, preferred_element_type=F32).astype(BF).astype(F32)
            unstack(oc, i, b, out_t.T.astype(BF))
            delta = jnp.sum(gs.astype(F32).T * out_t, axis=0, keepdims=True)
            dprob = lax.dot_general(vpad[rows, :], gs, NT, preferred_element_type=F32)
            dscore = (low.astype(F32) * (dprob - delta)).astype(BF)
            dq_t = jnp.dot(kt[b, :, window], dscore, preferred_element_type=F32)
            unstack(dqc, i, b, (dq_t * SCALE).T.astype(BF))
            key_term = jnp.dot(dscore, qs, preferred_element_type=F32) * SCALE
            kvb[n, EDGE : EDGE + WIN, 0:HEAD] = key_term.astype(BF)
            kvb[n, EDGE : EDGE + WIN, HEAD:] = jnp.dot(low, gs, preferred_element_type=F32).astype(BF)
        push(me, home(oc, i), out_wide(att, me.head), o_s.at[i], o_r.at[me.core * 4 + me.head], me.par, i)

    def gather(out, half, n):
        tile_at = half * 4 + n

        @pl.loop(0, 4)
        def _(m):
            pieces = []
            for c in range(10):
                i, b = (tile_at + c // 2) % N_CTX, c % 2
                row = EDGE + BAND + (m - c // 2 * 4 - core * 2 - b) * BLOCK
                pieces.append(kvb[i * 2 + b, pl.ds(pl.multiple_of(row, BLOCK), BLOCK), :])
            pieces += pieces[0:2]
            step = tsv[par, pl.ds(tile_at * 4 + m, 1), :]
            pick = jnp.where(code[...] == step, 1.0, 0.0).astype(BF)
            sums = jnp.dot(pick, jnp.concatenate(pieces, axis=0), preferred_element_type=F32).astype(BF)
            dst = pl.ds(pl.multiple_of(n * TOK + m * BLOCK, BLOCK), BLOCK)
            for t in range(N_CTX):
                out[0, t, dst, :] = sums[t * BLOCK : (t + 1) * BLOCK, 0:HEAD]
                out[1, t, dst, :] = sums[t * BLOCK : (t + 1) * BLOCK, HEAD:]

    def rows_of(n):
        return pl.ds(n * TOK, TOK)

    swaps = []
    for n in range(4):
        gather(away_t, 1 - core, n)
        swaps.append(
            remote(away_t.at[:, :, rows_of(n), :], part.at[:, :, rows_of(n), :], sw_s.at[n], sw_r.at[n], me.partner)
        )
        swaps[n].start()

    def tile(ref, n):
        return ref.at[rows_of(n), :]

    v_core = me.head // 2
    v_col = pl.multiple_of(me.head % 2 * HEAD, HEAD)
    k_col = pl.multiple_of(me.head * HEAD, HEAD)
    v_dst = dv_pair.at[pl.ds(pl.multiple_of(me.par * TOK, TOK), TOK), pl.ds(v_col, HEAD)]
    k_dst = dko.at[:, pl.ds(k_col, HEAD)]
    for n in range(4):
        gather(own_t, core, n)
        swaps[n].wait_recv()

        @pl.loop(0, 2)
        def _(m, n=n):
            rows = pl.ds(pl.multiple_of(n * TOK + m * DROWS, DROWS), DROWS)
            noise = jit[rows, :]
            for f, out in ((0, kd), (1, vd)):
                acc = jnp.zeros((DROWS, HEAD), F32)
                for t in range(N_CTX):
                    total = acc + (own_t[f, t, rows, :].astype(F32) + part[f, t, rows, :].astype(F32))
                    u = noise[:, f * 8 + t : f * 8 + t + 1]
                    acc = (total + u * jnp.abs(total)).astype(BF).astype(F32)
                out[rows, :] = acc.astype(BF)

        push(me, tile(vd, n), v_dst, dv_s.at[n], dv_r.at[me.par * 2 + me.head % 2], v_core, me.core * 4 + n)
    for n in range(4):
        landed(dv_pair.at[pl.ds(n // 2 * TOK, TOK), pl.ds(n % 2 * HEAD, HEAD)], dv_r.at[n])

    def sub_ylo(sub):
        return 1 - me.ylo if sub == 0 else me.ylo

    def local_sum(z, ylo):
        col = pl.multiple_of(ylo * 2048 + z * 256, 256)
        return lax.dot_general(
            xv[:, :, pl.ds(col, 256)].reshape(2 * TOK, 256), dv_pair[...], TN, preferred_element_type=F32
        )

    ways = ((1, up_b, up_in, ru_s, ru_r, me.up), (-1, dn_b, dn_in, rd_s, rd_r, me.down))

    def sums(w, s, sub):
        _, buf, inn, ssem, rsem, to = ways[w]
        n = s * 2 + sub
        return remote(buf.at[n], inn.at[n], ssem.at[n], rsem.at[n], to)

    travel = {}

    def step(w, s, sub):
        sign, buf, inn = ways[w][:3]
        n = s * 2 + sub
        total = local_sum((me.z + N_Z + sign * (4 - s)) % N_Z, sub_ylo(sub))
        if (w, s - 1, sub) in travel:
            travel[w, s - 1, sub].wait_recv()
            total = total + inn[n - 2].astype(F32)
        buf[n] = total.astype(BF)
        travel[w, s, sub] = sums(w, s, sub)
        travel[w, s, sub].start()

    step(0, 0, 0)
    step(1, 0, 1)

    for i in range(N_CTX):
        push(me, home(dqc, i), out_wide(dqo, me.head), d_s.at[i], d_r.at[me.core * 4 + me.head], me.par, i)
    for n in range(4):
        push(me, tile(kd, n), k_dst, dk_s.at[n], dk_r.at[me.head], me.par, me.core * 4 + n)

    for s in range(1, 4):
        for sub in range(2):
            step(0, s, sub)
            step(1, s, sub)

    def finish(sub):
        total = local_sum(me.z, sub_ylo(sub))
        for w in range(2):
            travel[w, 3, sub].wait_recv()
            total = total + ways[w][2][6 + sub].astype(F32)
        return total

    y_b[...] = finish(0).astype(BF)
    over = remote(y_b, y_in, one_s.at[5], one_r.at[5], me.across)
    over.start()
    wsum[...] = finish(1)
    over.wait()
    c_b[...] = (wsum[...] + y_in[...].astype(F32)).astype(BF)
    for n in range(16):
        push(
            me, c_b.at[pl.ds(n * 16, 16), :], c_in.at[me.core, me.ctx], c_s.at[n], c_r.at[me.core * N_CTX + me.ctx],
            n // N_CTX, n % N_CTX,
        )
    for n in range(16):
        landed(c_in.at[n // N_CTX, n % N_CTX], c_r.at[n])
    for half in range(2):
        total = c_in[half, 0].astype(F32)
        for i in range(1, N_CTX):
            total = total + c_in[half, i].astype(F32)
        wg[:, half * COLS : (half + 1) * COLS] = total

    for copies in started.values():
        for copy in copies:
            copy.wait_send()
    for n, (to, ctx) in enumerate(plane):
        pushed(me, w_src(to), w_s.at[n], to, ctx)
    for n in range(8):
        to, j = n // 4, n % 4
        pushed(me, k_src(j), k_s.at[n], to, me.core * 4 + j)
        pushed(me, wide(q, to, j), q_s.at[n], to, me.core * 4 + j)
        pushed(me, wide(g, to, j), g_s.at[n], to, me.core * 4 + j)
    for n, (to, p, jj) in enumerate(routes):
        pushed(me, v_src(p, jj), v_s.at[n], to, p * 4 + me.core * 2 + jj)
    for n in range(4):
        swaps[n].wait_send()
    for copy in travel.values():
        copy.wait_send()
    for n in range(16):
        pushed(me, c_b.at[pl.ds(n * 16, 16), :], c_s.at[n], n // N_CTX, n % N_CTX)
    for n in range(4):
        pushed(me, tile(vd, n), dv_s.at[n], v_core, me.core * 4 + n)
        pushed(me, tile(kd, n), dk_s.at[n], me.par, me.core * 4 + n)
        landed(dko.at[:, pl.ds(n * HEAD, HEAD)], dk_r.at[n])
    for i in range(N_CTX):
        pushed(me, home(oc, i), o_s.at[i], me.par, i)
        pushed(me, home(dqc, i), d_s.at[i], me.par, i)
    for n in range(8):
        dst = (pl.ds(n // 4 * HALF, HALF), pl.ds(n % 4 * GROUP * HEAD, GROUP * HEAD))
        landed(att.at[dst], o_r.at[n])
        landed(dqo.at[dst], d_r.at[n])


def run(q, g, k, x, w, lens, plc, tsel, bits):
    slab = (256, COLS)
    rows = (SEQ // 2, GROUP * HEAD)
    table = (2, N_CTX, SEQ // 2, HEAD)
    return pl.pallas_call(
        kernel,
        out_shape=[
            jax.ShapeDtypeStruct((TOK, D), BF),
            jax.ShapeDtypeStruct((TOK, D), BF),
            jax.ShapeDtypeStruct((TOK, KVW), BF),
            jax.ShapeDtypeStruct((16, KVW), F32),
        ],
        in_specs=[ANY] * 9,
        out_specs=[ANY] * 3 + [pl.BlockSpec(memory_space=pltpu.VMEM)],
        scratch_shapes=[
            vmem((2, N_Z, 256, COLS), BF), vmem((2, TOK, D), BF), vmem((2 * TOK, COLS), BF), vmem((2 * TOK, COLS), F32),
            vmem(rows, BF), vmem(rows, BF), vmem(rows, BF), vmem(rows, BF),
            vmem((PAD_ROWS, HEAD), BF), vmem((PAD_ROWS, HEAD), BF), vmem((2, HEAD, 1536), BF), vmem((2, HEAD, 1536), BF),
            vmem((2,) + lens.shape, I32), vmem((2,) + plc.shape, I32),
            vmem(bits.shape, I32), vmem((SEQ // 2, HEAD), F32), vmem(tsel.shape, I32), vmem((N_CTX * BLOCK, CAND * BLOCK), I32),
            vmem((16, WIN, GROUP * BLOCK), BF), vmem((16, SPAN, 2 * HEAD), BF),
            vmem(table, BF), vmem(table, BF), vmem(table, BF),
            vmem((2 * TOK, COLS), BF), vmem((SEQ // 2, HEAD), BF), vmem((SEQ // 2, HEAD), BF),
            vmem((8,) + slab, BF), vmem((8,) + slab, BF), vmem((8,) + slab, BF), vmem((8,) + slab, BF),
            vmem(slab, BF), vmem(slab, BF), vmem(slab, BF), vmem((2, N_CTX, 16, COLS), BF), vmem(slab, F32),
            dma(16), dma(16), dma(8), dma(8), dma(8), dma(8), dma(8), dma(8), dma(8), dma(8),
            dma(6), dma(6), dma(4 * SUBS), dma(4 * SUBS), dma(4 * SUBS), dma(4 * SUBS), dma(5),
            dma(4), dma(4), dma(8), dma(8), dma(8), dma(8), dma(4), dma(4), dma(4), dma(4),
            dma(8), dma(8), dma(8), dma(8), dma(16), dma(16),
        ],
        compiler_params=pltpu.CompilerParams(
            collective_id=0, has_side_effects=True, vmem_limit_bytes=60 * 2**20
        ),
        cost_estimate=pl.CostEstimate(flops=6 * 10**9, bytes_accessed=16 * 2**20, transcendentals=2 * 10**6),
        name="cycle",
    )(q, g, k, x, w, lens, plc, tsel, bits)


def move_kernel(*refs):
    for n in range(4):
        refs[4 + n][...] = refs[n][...]


def move(arrays):
    steps = 2
    specs = [pl.BlockSpec((a.shape[0] // steps, a.shape[1]), lambda i: (i, 0)) for a in arrays]
    return pl.pallas_call(
        move_kernel,
        grid=(steps,),
        out_shape=[jax.ShapeDtypeStruct(a.shape, a.dtype) for a in arrays],
        in_specs=specs,
        out_specs=specs,
        compiler_params=pltpu.CompilerParams(vmem_limit_bytes=60 * 2**20),
        name="move",
    )(*arrays)


def local(queries, key_vectors, activations, value_weight, attended_grad, doc_ids, shard_plan, round_bits):
    docs = jnp.arange(16, dtype=I32)
    starts = jnp.sum((doc_ids < docs[:, None]).astype(I32), axis=1)
    first = jnp.sum(jnp.where(doc_ids == docs[:, None], starts[:, None], 0), axis=0)
    earlier = (jnp.arange(SEQ, dtype=I32) - first).reshape(SEQ // BLOCK, BLOCK)
    lens = jnp.tile(earlier, (1, GROUP))
    blocks = jnp.arange(SEQ // BLOCK, dtype=I32)
    plan = shard_plan[0]
    place = jnp.sum(jnp.where(plan[:, None] == blocks[None, :], blocks[:, None], 0), axis=0)
    token = jnp.arange(SEQ, dtype=I32)
    token_place = jnp.sum(jnp.where(plan[:, None] == token[None, :] // BLOCK, blocks[:, None], 0), axis=0)
    plc = jnp.broadcast_to((token_place * BLOCK + token % BLOCK)[None, :], (8, SEQ))
    shape = (2, SEQ // BLOCK, CAND * BLOCK)
    core, key_block, col = [lax.broadcasted_iota(I32, shape, n) for n in range(3)]
    cand = col // BLOCK
    query_block = (key_block // 4 + cand // 2) * 4 + core * 2 + cand % 2
    ahead = query_block - key_block
    seen = (cand < 10) & (query_block < SEQ // BLOCK) & (ahead >= 0) & (ahead <= BAND // BLOCK)
    hit = query_block[..., None] == plan
    owner = jnp.sum(jnp.where(hit, blocks // 4, 0), axis=-1)
    step = (owner - (place // 4)[None, :, None]) % N_CTX
    tsel = jnp.where(seen, step, -1)
    bits = round_bits.transpose(0, 2, 1).reshape(N_CTX * 8, SEQ)
    outs = run(
        queries[0], attended_grad[0], key_vectors[0], activations[0], value_weight, lens, plc, tsel, bits
    )
    att, dqo, dko, wg = move(outs)
    return att[None], dqo[None], dko[None], wg


def solution(mesh):
    rows = P("dp", "ctx", None)
    every = P(("dp", "ctx"), None)
    return jax.shard_map(
        local,
        mesh=mesh,
        in_specs=(rows, rows, rows, every, rows, P("dp", None), P("dp", None), P()),
        out_specs=(rows, rows, rows, every),
        check_vma=False,
    )
```

```python
import functools

import jax
import jax.numpy as jnp
from jax import lax
from jax.experimental import pallas as pl
from jax.experimental.pallas import tpu as pltpu
from jax.sharding import PartitionSpec as P

MESH = pl.DeviceIdType.MESH
ANY = pl.BlockSpec(memory_space=pl.ANY)
BF = jnp.bfloat16
F32 = jnp.float32
I32 = jnp.int32

N_CTX = 8
N_Z = 8
HEAD = 128
GROUP = 8
TOK = 128
HALF = 64
SEQ = 1024
BLOCK = 32
BAND = 512
WIN = BAND + BLOCK
D = 4096
KVW = 512
COLS = 256
PAD_ROWS = SEQ + BAND + 128
SCALE = HEAD**-0.5
LOG2E = 1.4426950408889634
NEG = -1e30
SUBS = 2
SUB_ROWS = 512 // SUBS
DROWS = 64
EDGE = 3 * BLOCK
SPAN = WIN + 2 * EDGE
CAND = 12

NT = (((1,), (1,)), ((), ()))
TN = (((0,), (0,)), ((), ()))


def vmem(shape, dtype):
    return pltpu.VMEM(shape, dtype)


def dma(*shape):
    return pltpu.SemaphoreType.DMA(shape)


class Place:
    def __init__(self):
        self.dp = lax.axis_index("dp")
        self.ctx = lax.axis_index("ctx")
        self.core = self.dp % 2
        self.z = (self.dp // 2) % N_Z
        self.ylo = self.dp // 16
        self.base = self.dp - self.core
        self.par = self.ctx // 4
        self.head = self.ctx % 4
        self.partner = (self.base + 1 - self.core, self.ctx)
        self.across = (self.dp + 16 - 32 * self.ylo, self.ctx)
        self.up = (self.ylo * 16 + (self.z + 1) % N_Z * 2 + self.core, self.ctx)
        self.down = (self.ylo * 16 + (self.z + N_Z - 1) % N_Z * 2 + self.core, self.ctx)

    def is_me(self, core, ctx):
        return (self.core == core) & (self.ctx == ctx)


def greet(me):
    barrier = pltpu.get_barrier_semaphore()
    for core in range(2):
        for ctx in range(N_CTX):

            @pl.when(jnp.logical_not(me.is_me(core, ctx)))
            def _(core=core, ctx=ctx):
                pl.semaphore_signal(barrier, inc=1, device_id=(me.base + core, jnp.int32(ctx)), device_id_type=MESH)

    for other in (me.across, me.up, me.down):
        pl.semaphore_signal(barrier, inc=1, device_id=other, device_id_type=MESH)
    pl.semaphore_wait(barrier, 2 * N_CTX + 2)


def remote(src, dst, ssem, rsem, device):
    return pltpu.make_async_remote_copy(
        src_ref=src, dst_ref=dst, send_sem=ssem, recv_sem=rsem, device_id=device, device_id_type=MESH
    )


def push(me, src, dst, ssem, rsem, core, ctx):
    mine = me.is_me(core, ctx)

    @pl.when(mine)
    def _():
        pltpu.make_async_copy(src, dst, rsem).start()

    @pl.when(jnp.logical_not(mine))
    def _():
        remote(src, dst, ssem, rsem, (me.base + core, jnp.int32(ctx))).start()


def pushed(me, src, ssem, core, ctx):
    @pl.when(jnp.logical_not(me.is_me(core, ctx)))
    def _():
        remote(src, src, ssem, ssem, (me.base + core, jnp.int32(ctx))).wait_send()


def landed(dst, rsem):
    pltpu.make_async_copy(dst, dst, rsem).wait()


def kernel(
    q, g, k, x, w, docs, plan, bits, att, dqo, dko, wg,
    wfull, xv, vbuf, vacc, qa, ga, oc, dqc, kpad, vpad, kt, vt, docv, planv, planrow, firstv, bitv, jit,
    tsv, code, pst, kvb, away_t, own_t, part, dv_pair, kd, vd,
    up_b, dn_b, up_in, dn_in, y_b, y_in, c_b, c_in, wsum,
    w_s, w_r, q_s, q_r, g_s, g_r, k_s, k_r, v_s, v_r, one_s, one_r, up_s, up_r, dn_s, dn_r, loc,
    sw_s, sw_r, o_s, o_r, d_s, d_r, dk_s, dk_r, dv_s, dv_r, ru_s, ru_r, rd_s, rd_r, c_s, c_r,
):
    me = Place()
    core, par = me.core, me.par
    for pad in (kpad, vpad):
        pad[0:BAND, :] = jnp.zeros((BAND, HEAD), BF)
        pad[BAND + SEQ :, :] = jnp.zeros((PAD_ROWS - BAND - SEQ, HEAD), BF)
    kvb[:, 0:EDGE, :] = jnp.zeros((16, EDGE, 2 * HEAD), BF)
    kvb[:, EDGE + WIN :, :] = jnp.zeros((16, EDGE, 2 * HEAD), BF)
    down = lax.broadcasted_iota(I32, code.shape, 0)
    right = lax.broadcasted_iota(I32, code.shape, 1)
    code[...] = jnp.where(down % BLOCK == right % BLOCK, down // BLOCK, N_CTX)
    vacc[...] = jnp.zeros_like(vacc)
    greet(me)
    plane = [(n // N_CTX, n % N_CTX) for n in range(2 * N_CTX)]

    def w_src(core):
        return w.at[:, pl.ds(core * COLS, COLS)]

    row = pl.multiple_of(me.core * 128 + me.ctx * 16, 16)
    w_dst = wfull.at[me.ylo, me.z, pl.ds(row, 16), :]
    for n, (to, ctx) in enumerate(plane):
        push(me, w_src(to), w_dst, w_s.at[n], w_r.at[me.core * N_CTX + me.ctx], to, ctx)

    own_x = pltpu.make_async_copy(x, xv.at[me.core], loc.at[0])
    own_l = pltpu.make_async_copy(docs, docv.at[me.core], loc.at[1])
    own_p = pltpu.make_async_copy(plan, planv.at[me.core], loc.at[2])
    far_x = remote(x, xv.at[me.core], one_s.at[0], one_r.at[0], me.partner)
    far_l = remote(docs, docv.at[me.core], one_s.at[1], one_r.at[1], me.partner)
    far_p = remote(plan, planv.at[me.core], one_s.at[2], one_r.at[2], me.partner)
    bits_in = pltpu.make_async_copy(bits, bitv, loc.at[3])
    for copy in (own_x, far_x, own_l, far_l, own_p, far_p, bits_in):
        copy.start()

    def k_src(j):
        return k.at[:, pl.ds(j * HEAD, HEAD)]

    def wide(ref, core, j):
        return ref.at[pl.ds(core * HALF, HALF), pl.ds(j * GROUP * HEAD, GROUP * HEAD)]

    spot = pl.multiple_of(BAND + me.ctx * TOK, TOK)
    half_spot = pl.multiple_of(me.ctx * HALF, HALF)

    for n in range(8):
        to, j = n // 4, n % 4
        push(me, k_src(j), kpad.at[pl.ds(spot, TOK), :], k_s.at[n], k_r.at[me.ctx], to, me.core * 4 + j)
    for n in range(16):
        landed(wfull.at[me.ylo, me.z, pl.ds(n * 16, 16), :], w_r.at[n])
    mine = wfull.at[me.ylo, me.z]
    over = remote(mine, mine, one_s.at[3], one_r.at[3], me.across)
    over.start()

    def piece(z, sub):
        ylo = me.ylo if sub < SUBS // 2 else 1 - me.ylo
        return wfull.at[ylo, z, pl.ds(sub % (SUBS // 2) * SUB_ROWS, SUB_ROWS), :]

    def ring(s, sub):
        z_up, z_dn = (me.z + N_Z - s) % N_Z, (me.z + s) % N_Z
        n = s * SUBS + sub
        up = remote(piece(z_up, sub), piece(z_up, sub), up_s.at[n], up_r.at[n], me.up)
        dn = remote(piece(z_dn, sub), piece(z_dn, sub), dn_s.at[n], dn_r.at[n], me.down)
        half = up if sub % 2 == 0 else dn
        return [up, dn] if s < 3 else [half]

    started = {}

    def go(s, sub):
        started[s, sub] = ring(s, sub)
        for copy in started[s, sub]:
            copy.start()

    for sub in range(SUBS // 2):
        go(0, sub)
    for n in range(8):
        to, j = n // 4, n % 4
        push(me, wide(q, to, j), qa.at[pl.ds(half_spot, HALF), :], q_s.at[n], q_r.at[me.ctx], to, me.core * 4 + j)
    for n in range(8):
        to, j = n // 4, n % 4
        push(me, wide(g, to, j), ga.at[pl.ds(half_spot, HALF), :], g_s.at[n], g_r.at[me.ctx], to, me.core * 4 + j)
    own_x.wait()
    far_x.wait()
    over.wait()
    for sub in range(SUBS // 2, SUBS):
        go(0, sub)

    def project(z):
        for ylo in range(2):
            col = pl.multiple_of(ylo * 2048 + z * 256, 256)
            part = xv[:, :, pl.ds(col, 256)].reshape(2 * TOK, 256)
            vacc[...] += jnp.dot(part, wfull[ylo, z], preferred_element_type=F32)

    def transposed(out, pad):
        for b in range(2):
            for n in range(12):
                rows = pl.ds(pl.multiple_of(core * HALF + b * BLOCK + n * 128, BLOCK), 128)
                out[b, :, n * 128 : n * 128 + 128] = pad[rows, :].T

    def stacked(ref, i, b):
        rows = pl.ds(pl.multiple_of(i * HALF + b * BLOCK, BLOCK), BLOCK)
        return jnp.concatenate([ref[rows, h * HEAD : (h + 1) * HEAD] for h in range(GROUP)], axis=0)

    def unstack(ref, i, b, value):
        rows = pl.ds(pl.multiple_of(i * HALF + b * BLOCK, BLOCK), BLOCK)
        for h in range(GROUP):
            ref[rows, h * HEAD : (h + 1) * HEAD] = value[h * BLOCK : (h + 1) * BLOCK]

    def keys_of(i, b):
        block = i * 4 + core * 2 + b
        return block, pl.ds(pl.multiple_of(block * BLOCK, BLOCK), WIN)

    key_row = lax.broadcasted_iota(I32, (WIN, GROUP * BLOCK), 0)
    lane = lax.broadcasted_iota(I32, (1, GROUP * BLOCK), 1) % BLOCK

    def iota(shape, axis):
        return lax.broadcasted_iota(I32, shape, axis)

    def tables():
        doc = docv[par]
        first = jnp.zeros(doc.shape, I32)
        for d in range(15):
            size = jnp.sum(jnp.where(doc == d, 1, 0), axis=1, keepdims=True)
            first = first + jnp.where(doc > d, size, 0)
        first = jnp.broadcast_to(first, (SEQ // BLOCK, SEQ))
        mine = iota(first.shape, 0) == iota(first.shape, 1) // BLOCK
        same = iota((SEQ, GROUP * BLOCK), 0) % BLOCK == iota((SEQ, GROUP * BLOCK), 1) % BLOCK
        same = jnp.where(same, 1.0, 0.0).astype(BF)
        spread = []
        for part in (first // BLOCK, first % BLOCK):
            part = jnp.where(mine, part, 0).astype(F32).astype(BF)
            spread.append(jnp.dot(part, same, preferred_element_type=F32).astype(I32))
        firstv[...] = spread[0] * BLOCK + spread[1]

        plan = planv[par]
        block = iota((1, SEQ), 1) // BLOCK
        key_block, col = iota(tsv.shape, 0), iota(tsv.shape, 1)
        cand = col // BLOCK
        query_block = (key_block // 4 + cand // 2) * 4 + core * 2 + cand % 2
        place = jnp.zeros((1, SEQ), I32)
        step = jnp.zeros(tsv.shape, I32)
        for p in range(SEQ // BLOCK):
            at = plan[:, p : p + 1]
            place = place + jnp.where(block == at, p, 0)
            step = step + jnp.where(query_block == at, p // 4, 0) - jnp.where(key_block == at, p // 4, 0)
        step = jnp.where(step < 0, step + N_CTX, step)
        ahead = query_block - key_block
        seen = (cand < 10) & (query_block < SEQ // BLOCK) & (ahead >= 0) & (ahead <= BAND // BLOCK)
        tsv[...] = jnp.where(seen, step, -1)
        planrow[...] = place * BLOCK + iota((1, SEQ), 1) % BLOCK

    def scores(low, high):
        @pl.loop(low, high)
        def _(i):
            landed(qa.at[pl.ds(pl.multiple_of(i * HALF, HALF), HALF), :], q_r.at[i])
            for b in range(2):
                block, rows = keys_of(i, b)
                first = firstv[pl.ds(block, 1), :] + (BAND - block * BLOCK)
                allowed = (key_row >= first) & (key_row <= lane + BAND)
                s = lax.dot_general(kpad[rows, :], stacked(qa, i, b), NT, preferred_element_type=F32)
                s = jnp.where(allowed, s * (SCALE * LOG2E), NEG)
                weight = jnp.exp2(s - jnp.max(s, axis=0, keepdims=True))
                prob = weight * (1.0 / jnp.sum(weight, axis=0, keepdims=True))
                pst[i * 2 + b] = prob.astype(BF)

    for s in range(1, 4):
        for sub in range(SUBS):
            up, dn = started[s - 1, sub]
            up.wait_recv()
            dn.wait_recv()
            go(s, sub)
        project((me.z + N_Z - s + 1) % N_Z)
        if s > 1:
            project((me.z + s - 1) % N_Z)
    for i in range(N_CTX):
        landed(kpad.at[pl.ds(BAND + i * TOK, TOK), :], k_r.at[i])
    transposed(kt, kpad)
    for copy in (own_l, far_l, own_p, far_p):
        copy.wait()
    tables()
    project((me.z + N_Z - 3) % N_Z)
    project((me.z + 3) % N_Z)
    scores(0, 3)
    for sub in range(SUBS):
        started[3, sub][0].wait_recv()
    project((me.z + N_Z - 4) % N_Z)

    vbuf[...] = vacc[...].astype(BF)

    def v_src(p, jj):
        return vbuf.at[pl.ds(p * TOK, TOK), pl.ds(jj * HEAD, HEAD)]

    routes = [(n // 4, n // 2 % 2, n % 2) for n in range(8)]
    for n, (to, p, jj) in enumerate(routes):
        push(
            me, v_src(p, jj), vpad.at[pl.ds(spot, TOK), :], v_s.at[n], v_r.at[me.ctx], to, p * 4 + me.core * 2 + jj
        )
    scores(3, N_CTX)
    bits_in.wait()
    wanted = [bitv[pl.ds(t * 8 + f * 4 + me.head, 1), :] for f in range(2) for t in range(N_CTX)]
    jitter = (jnp.concatenate(wanted, axis=0).astype(F32) * 2.0**-30 - 0.5) * 2.0**-4
    parts = []
    for _ in range(3):
        parts.append(jitter.astype(BF))
        jitter = jitter - parts[-1].astype(F32)
    at = planrow[:, pl.ds(pl.multiple_of(core * (SEQ // 2), SEQ // 2), SEQ // 2)]
    there = lax.broadcasted_iota(I32, (SEQ, SEQ // 2), 0) == at
    moved = jnp.dot(
        jnp.concatenate(parts, axis=0), jnp.where(there, 1.0, 0.0).astype(BF), preferred_element_type=F32
    )
    moved = moved[0:16] + moved[16:32] + moved[32:48]
    jit[...] = jnp.concatenate([moved, jnp.zeros((112, SEQ // 2), F32)], axis=0).T
    for i in range(N_CTX):
        landed(vpad.at[pl.ds(BAND + i * TOK, TOK), :], v_r.at[i])
    transposed(vt, vpad)

    def out_wide(ref, j):
        cols = pl.ds(pl.multiple_of(j * GROUP * HEAD, HEAD), GROUP * HEAD)
        return ref.at[pl.ds(pl.multiple_of(me.core * HALF, HALF), HALF), cols]

    def home(ref, i):
        return ref.at[pl.ds(pl.multiple_of(i * HALF, HALF), HALF), :]

    @pl.loop(0, N_CTX)
    def _(i):
        landed(home(ga, i), g_r.at[i])
        window = pl.ds(pl.multiple_of(i * TOK, TOK), WIN)
        for b in range(2):
            n = i * 2 + b
            _, rows = keys_of(i, b)
            low, qs, gs = pst[n], stacked(qa, i, b), stacked(ga, i, b)
            out_t = jnp.dot(vt[b, :, window], low, preferred_element_type=F32).astype(BF).astype(F32)
            unstack(oc, i, b, out_t.T.astype(BF))
            delta = jnp.sum(gs.astype(F32).T * out_t, axis=0, keepdims=True)
            dprob = lax.dot_general(vpad[rows, :], gs, NT, preferred_element_type=F32)
            dscore = (low.astype(F32) * (dprob - delta)).astype(BF)
            dq_t = jnp.dot(kt[b, :, window], dscore, preferred_element_type=F32)
            unstack(dqc, i, b, (dq_t * SCALE).T.astype(BF))
            key_term = jnp.dot(dscore, qs, preferred_element_type=F32) * SCALE
            kvb[n, EDGE : EDGE + WIN, 0:HEAD] = key_term.astype(BF)
            kvb[n, EDGE : EDGE + WIN, HEAD:] = jnp.dot(low, gs, preferred_element_type=F32).astype(BF)
        push(me, home(oc, i), out_wide(att, me.head), o_s.at[i], o_r.at[me.core * 4 + me.head], me.par, i)

    def gather(out, half, n):
        tile_at = half * 4 + n

        @pl.loop(0, 4)
        def _(m):
            pieces = []
            for c in range(10):
                i, b = (tile_at + c // 2) % N_CTX, c % 2
                row = EDGE + BAND + (m - c // 2 * 4 - core * 2 - b) * BLOCK
                pieces.append(kvb[i * 2 + b, pl.ds(pl.multiple_of(row, BLOCK), BLOCK), :])
            pieces += pieces[0:2]
            step = tsv[pl.ds(tile_at * 4 + m, 1), :]
            pick = jnp.where(code[...] == step, 1.0, 0.0).astype(BF)
            sums = jnp.dot(pick, jnp.concatenate(pieces, axis=0), preferred_element_type=F32).astype(BF)
            dst = pl.ds(pl.multiple_of(n * TOK + m * BLOCK, BLOCK), BLOCK)
            for t in range(N_CTX):
                out[0, t, dst, :] = sums[t * BLOCK : (t + 1) * BLOCK, 0:HEAD]
                out[1, t, dst, :] = sums[t * BLOCK : (t + 1) * BLOCK, HEAD:]

    def rows_of(n):
        return pl.ds(n * TOK, TOK)

    swaps = []
    for n in range(4):
        gather(away_t, 1 - core, n)
        swaps.append(
            remote(away_t.at[:, :, rows_of(n), :], part.at[:, :, rows_of(n), :], sw_s.at[n], sw_r.at[n], me.partner)
        )
        swaps[n].start()

    def tile(ref, n):
        return ref.at[rows_of(n), :]

    v_core = me.head // 2
    v_col = pl.multiple_of(me.head % 2 * HEAD, HEAD)
    k_col = pl.multiple_of(me.head * HEAD, HEAD)
    v_dst = dv_pair.at[pl.ds(pl.multiple_of(me.par * TOK, TOK), TOK), pl.ds(v_col, HEAD)]
    k_dst = dko.at[:, pl.ds(k_col, HEAD)]
    for n in range(4):
        gather(own_t, core, n)
        swaps[n].wait_recv()

        @pl.loop(0, 2)
        def _(m, n=n):
            rows = pl.ds(pl.multiple_of(n * TOK + m * DROWS, DROWS), DROWS)
            noise = jit[rows, :]
            for f, out in ((0, kd), (1, vd)):
                acc = jnp.zeros((DROWS, HEAD), F32)
                for t in range(N_CTX):
                    total = acc + (own_t[f, t, rows, :].astype(F32) + part[f, t, rows, :].astype(F32))
                    u = noise[:, f * 8 + t : f * 8 + t + 1]
                    acc = (total + u * jnp.abs(total)).astype(BF).astype(F32)
                out[rows, :] = acc.astype(BF)

        push(me, tile(vd, n), v_dst, dv_s.at[n], dv_r.at[me.par * 2 + me.head % 2], v_core, me.core * 4 + n)
    for n in range(4):
        landed(dv_pair.at[pl.ds(n // 2 * TOK, TOK), pl.ds(n % 2 * HEAD, HEAD)], dv_r.at[n])

    def sub_ylo(sub):
        return 1 - me.ylo if sub == 0 else me.ylo

    def local_sum(z, ylo):
        col = pl.multiple_of(ylo * 2048 + z * 256, 256)
        return lax.dot_general(
            xv[:, :, pl.ds(col, 256)].reshape(2 * TOK, 256), dv_pair[...], TN, preferred_element_type=F32
        )

    ways = ((1, up_b, up_in, ru_s, ru_r, me.up), (-1, dn_b, dn_in, rd_s, rd_r, me.down))

    def sums(w, s, sub):
        _, buf, inn, ssem, rsem, to = ways[w]
        n = s * 2 + sub
        return remote(buf.at[n], inn.at[n], ssem.at[n], rsem.at[n], to)

    travel = {}

    def step(w, s, sub):
        sign, buf, inn = ways[w][:3]
        n = s * 2 + sub
        total = local_sum((me.z + N_Z + sign * (4 - s)) % N_Z, sub_ylo(sub))
        if (w, s - 1, sub) in travel:
            travel[w, s - 1, sub].wait_recv()
            total = total + inn[n - 2].astype(F32)
        buf[n] = total.astype(BF)
        travel[w, s, sub] = sums(w, s, sub)
        travel[w, s, sub].start()

    step(0, 0, 0)
    step(1, 0, 1)

    for i in range(N_CTX):
        push(me, home(dqc, i), out_wide(dqo, me.head), d_s.at[i], d_r.at[me.core * 4 + me.head], me.par, i)
    for n in range(4):
        push(me, tile(kd, n), k_dst, dk_s.at[n], dk_r.at[me.head], me.par, me.core * 4 + n)

    for s in range(1, 4):
        for sub in range(2):
            step(0, s, sub)
            step(1, s, sub)

    def finish(sub):
        total = local_sum(me.z, sub_ylo(sub))
        for w in range(2):
            travel[w, 3, sub].wait_recv()
            total = total + ways[w][2][6 + sub].astype(F32)
        return total

    y_b[...] = finish(0).astype(BF)
    over = remote(y_b, y_in, one_s.at[5], one_r.at[5], me.across)
    over.start()
    wsum[...] = finish(1)
    over.wait()
    c_b[...] = (wsum[...] + y_in[...].astype(F32)).astype(BF)
    for n in range(16):
        push(
            me, c_b.at[pl.ds(n * 16, 16), :], c_in.at[me.core, me.ctx], c_s.at[n], c_r.at[me.core * N_CTX + me.ctx],
            n // N_CTX, n % N_CTX,
        )
    for n in range(16):
        landed(c_in.at[n // N_CTX, n % N_CTX], c_r.at[n])
    for half in range(2):
        total = c_in[half, 0].astype(F32)
        for i in range(1, N_CTX):
            total = total + c_in[half, i].astype(F32)
        wg[:, half * COLS : (half + 1) * COLS] = total

    for copies in started.values():
        for copy in copies:
            copy.wait_send()
    for n, (to, ctx) in enumerate(plane):
        pushed(me, w_src(to), w_s.at[n], to, ctx)
    for n in range(8):
        to, j = n // 4, n % 4
        pushed(me, k_src(j), k_s.at[n], to, me.core * 4 + j)
        pushed(me, wide(q, to, j), q_s.at[n], to, me.core * 4 + j)
        pushed(me, wide(g, to, j), g_s.at[n], to, me.core * 4 + j)
    for n, (to, p, jj) in enumerate(routes):
        pushed(me, v_src(p, jj), v_s.at[n], to, p * 4 + me.core * 2 + jj)
    for n in range(4):
        swaps[n].wait_send()
    for copy in travel.values():
        copy.wait_send()
    for n in range(16):
        pushed(me, c_b.at[pl.ds(n * 16, 16), :], c_s.at[n], n // N_CTX, n % N_CTX)
    for n in range(4):
        pushed(me, tile(vd, n), dv_s.at[n], v_core, me.core * 4 + n)
        pushed(me, tile(kd, n), dk_s.at[n], me.par, me.core * 4 + n)
        landed(dko.at[:, pl.ds(n * HEAD, HEAD)], dk_r.at[n])
    for i in range(N_CTX):
        pushed(me, home(oc, i), o_s.at[i], me.par, i)
        pushed(me, home(dqc, i), d_s.at[i], me.par, i)
    for n in range(8):
        dst = (pl.ds(n // 4 * HALF, HALF), pl.ds(n % 4 * GROUP * HEAD, GROUP * HEAD))
        landed(att.at[dst], o_r.at[n])
        landed(dqo.at[dst], d_r.at[n])


def run(q, g, k, x, w, docs, plan, bits):
    slab = (256, COLS)
    rows = (SEQ // 2, GROUP * HEAD)
    table = (2, N_CTX, SEQ // 2, HEAD)
    return pl.pallas_call(
        kernel,
        out_shape=[
            jax.ShapeDtypeStruct((TOK, D), BF),
            jax.ShapeDtypeStruct((TOK, D), BF),
            jax.ShapeDtypeStruct((TOK, KVW), BF),
            jax.ShapeDtypeStruct((16, KVW), F32),
        ],
        in_specs=[ANY] * 8,
        out_specs=[ANY] * 3 + [pl.BlockSpec(memory_space=pltpu.VMEM)],
        scratch_shapes=[
            vmem((2, N_Z, 256, COLS), BF), vmem((2, TOK, D), BF), vmem((2 * TOK, COLS), BF), vmem((2 * TOK, COLS), F32),
            vmem(rows, BF), vmem(rows, BF), vmem(rows, BF), vmem(rows, BF),
            vmem((PAD_ROWS, HEAD), BF), vmem((PAD_ROWS, HEAD), BF), vmem((2, HEAD, 1536), BF), vmem((2, HEAD, 1536), BF),
            vmem((2,) + docs.shape, I32), vmem((2,) + plan.shape, I32), vmem(docs.shape, I32),
            vmem((SEQ // BLOCK, GROUP * BLOCK), I32),
            vmem(bits.shape, I32), vmem((SEQ // 2, HEAD), F32), vmem((SEQ // BLOCK, CAND * BLOCK), I32), vmem((N_CTX * BLOCK, CAND * BLOCK), I32),
            vmem((16, WIN, GROUP * BLOCK), BF), vmem((16, SPAN, 2 * HEAD), BF),
            vmem(table, BF), vmem(table, BF), vmem(table, BF),
            vmem((2 * TOK, COLS), BF), vmem((SEQ // 2, HEAD), BF), vmem((SEQ // 2, HEAD), BF),
            vmem((8,) + slab, BF), vmem((8,) + slab, BF), vmem((8,) + slab, BF), vmem((8,) + slab, BF),
            vmem(slab, BF), vmem(slab, BF), vmem(slab, BF), vmem((2, N_CTX, 16, COLS), BF), vmem(slab, F32),
            dma(16), dma(16), dma(8), dma(8), dma(8), dma(8), dma(8), dma(8), dma(8), dma(8),
            dma(6), dma(6), dma(4 * SUBS), dma(4 * SUBS), dma(4 * SUBS), dma(4 * SUBS), dma(5),
            dma(4), dma(4), dma(8), dma(8), dma(8), dma(8), dma(4), dma(4), dma(4), dma(4),
            dma(8), dma(8), dma(8), dma(8), dma(16), dma(16),
        ],
        compiler_params=pltpu.CompilerParams(
            collective_id=0, has_side_effects=True, vmem_limit_bytes=60 * 2**20
        ),
        cost_estimate=pl.CostEstimate(flops=6 * 10**9, bytes_accessed=16 * 2**20, transcendentals=2 * 10**6),
        name="cycle",
    )(q, g, k, x, w, docs, plan, bits)


def move_kernel(*refs):
    for n in range(4):
        refs[4 + n][...] = refs[n][...]


def move(arrays):
    steps = 2
    specs = [pl.BlockSpec((a.shape[0] // steps, a.shape[1]), lambda i: (i, 0)) for a in arrays]
    return pl.pallas_call(
        move_kernel,
        grid=(steps,),
        out_shape=[jax.ShapeDtypeStruct(a.shape, a.dtype) for a in arrays],
        in_specs=specs,
        out_specs=specs,
        compiler_params=pltpu.CompilerParams(vmem_limit_bytes=60 * 2**20),
        name="move",
    )(*arrays)


def local(queries, key_vectors, activations, value_weight, attended_grad, doc_ids, shard_plan, round_bits):
    bits = round_bits.transpose(0, 2, 1).reshape(N_CTX * 8, SEQ)
    outs = run(
        queries[0], attended_grad[0], key_vectors[0], activations[0], value_weight, doc_ids, shard_plan, bits
    )
    att, dqo, dko, wg = move(outs)
    return att[None], dqo[None], dko[None], wg


def solution(mesh):
    rows = P("dp", "ctx", None)
    every = P(("dp", "ctx"), None)
    return jax.shard_map(
        local,
        mesh=mesh,
        in_specs=(rows, rows, rows, every, rows, P("dp", None), P("dp", None), P()),
        out_specs=(rows, rows, rows, every),
        check_vma=False,
    )
```

```python
import functools

import jax
import jax.numpy as jnp
from jax import lax
from jax.experimental import pallas as pl
from jax.experimental.pallas import tpu as pltpu
from jax.sharding import PartitionSpec as P

MESH = pl.DeviceIdType.MESH
ANY = pl.BlockSpec(memory_space=pl.ANY)
BF = jnp.bfloat16
F32 = jnp.float32
I32 = jnp.int32

N_CTX = 8
N_Z = 8
HEAD = 128
GROUP = 8
TOK = 128
HALF = 64
SEQ = 1024
BLOCK = 32
BAND = 512
WIN = BAND + BLOCK
D = 4096
KVW = 512
COLS = 256
PAD_ROWS = SEQ + BAND + 128
SCALE = HEAD**-0.5
LOG2E = 1.4426950408889634
NEG = -1e30
SUBS = 2
SUB_ROWS = 512 // SUBS
DROWS = 64
EDGE = 3 * BLOCK
SPAN = WIN + 2 * EDGE
CAND = 12

NT = (((1,), (1,)), ((), ()))
TN = (((0,), (0,)), ((), ()))


def vmem(shape, dtype):
    return pltpu.VMEM(shape, dtype)


def dma(*shape):
    return pltpu.SemaphoreType.DMA(shape)


class Place:
    def __init__(self):
        self.dp = lax.axis_index("dp")
        self.ctx = lax.axis_index("ctx")
        self.core = self.dp % 2
        self.z = (self.dp // 2) % N_Z
        self.ylo = self.dp // 16
        self.base = self.dp - self.core
        self.par = self.ctx // 4
        self.head = self.ctx % 4
        self.partner = (self.base + 1 - self.core, self.ctx)
        self.up = (self.ylo * 16 + (self.z + 1) % N_Z * 2 + self.core, self.ctx)
        self.down = (self.ylo * 16 + (self.z + N_Z - 1) % N_Z * 2 + self.core, self.ctx)

    def over_there(self, core, ctx):
        return (self.base + 16 - 32 * self.ylo + core, jnp.int32(ctx))

    def is_me(self, core, ctx):
        return (self.core == core) & (self.ctx == ctx)


def greet(me):
    barrier = pltpu.get_barrier_semaphore()
    for ylo in range(2):
        for core in range(2):
            for ctx in range(N_CTX):

                @pl.when(jnp.logical_not((me.ylo == ylo) & me.is_me(core, ctx)))
                def _(ylo=ylo, core=core, ctx=ctx):
                    to = (ylo * 16 + me.z * 2 + core, jnp.int32(ctx))
                    pl.semaphore_signal(barrier, inc=1, device_id=to, device_id_type=MESH)

    for other in (me.up, me.down):
        pl.semaphore_signal(barrier, inc=1, device_id=other, device_id_type=MESH)
    pl.semaphore_wait(barrier, 4 * N_CTX + 1)


def remote(src, dst, ssem, rsem, device):
    return pltpu.make_async_remote_copy(
        src_ref=src, dst_ref=dst, send_sem=ssem, recv_sem=rsem, device_id=device, device_id_type=MESH
    )


def push(me, src, dst, ssem, rsem, core, ctx):
    mine = me.is_me(core, ctx)

    @pl.when(mine)
    def _():
        pltpu.make_async_copy(src, dst, rsem).start()

    @pl.when(jnp.logical_not(mine))
    def _():
        remote(src, dst, ssem, rsem, (me.base + core, jnp.int32(ctx))).start()


def pushed(me, src, ssem, core, ctx):
    @pl.when(jnp.logical_not(me.is_me(core, ctx)))
    def _():
        remote(src, src, ssem, ssem, (me.base + core, jnp.int32(ctx))).wait_send()


def landed(dst, rsem):
    pltpu.make_async_copy(dst, dst, rsem).wait()


def kernel(
    q, g, k, x, w, docs, plan, bits, att, dqo, dko, wg,
    wfull, xv, vbuf, vacc, qa, ga, oc, dqc, kpad, vpad, kt, vt, docv, planv, planrow, firstv, bitv, jit,
    tsv, code, pst, kvb, away_t, own_t, part, dv_pair, kd, vd,
    up_b, dn_b, up_in, dn_in, c_b, c_in,
    w_s, w_r, q_s, q_r, g_s, g_r, k_s, k_r, v_s, v_r, one_s, one_r, up_s, up_r, dn_s, dn_r, loc,
    sw_s, sw_r, o_s, o_r, d_s, d_r, dk_s, dk_r, dv_s, dv_r, ru_s, ru_r, rd_s, rd_r, c_s, c_r,
):
    me = Place()
    core, par = me.core, me.par
    for pad in (kpad, vpad):
        pad[0:BAND, :] = jnp.zeros((BAND, HEAD), BF)
        pad[BAND + SEQ :, :] = jnp.zeros((PAD_ROWS - BAND - SEQ, HEAD), BF)
    kvb[:, 0:EDGE, :] = jnp.zeros((16, EDGE, 2 * HEAD), BF)
    kvb[:, EDGE + WIN :, :] = jnp.zeros((16, EDGE, 2 * HEAD), BF)
    down = lax.broadcasted_iota(I32, code.shape, 0)
    right = lax.broadcasted_iota(I32, code.shape, 1)
    code[...] = jnp.where(down % BLOCK == right % BLOCK, down // BLOCK, N_CTX)
    vacc[...] = jnp.zeros_like(vacc)
    greet(me)
    plane = [(n // N_CTX, n % N_CTX) for n in range(2 * N_CTX)]

    def w_src(core):
        return w.at[:, pl.ds(core * COLS, COLS)]

    row = pl.multiple_of(me.core * 128 + me.ctx * 16, 16)
    w_dst = wfull.at[me.ylo, me.z, pl.ds(row, 16), :]
    for n, (to, ctx) in enumerate(plane):
        push(me, w_src(to), w_dst, w_s.at[n], w_r.at[me.core * N_CTX + me.ctx], to, ctx)
    for n, (to, ctx) in enumerate(plane):
        remote(w_src(to), w_dst, w_s.at[16 + n], w_r.at[16 + me.core * N_CTX + me.ctx], me.over_there(to, ctx)).start()

    own_x = pltpu.make_async_copy(x, xv.at[me.core], loc.at[0])
    own_l = pltpu.make_async_copy(docs, docv.at[me.core], loc.at[1])
    own_p = pltpu.make_async_copy(plan, planv.at[me.core], loc.at[2])
    far_x = remote(x, xv.at[me.core], one_s.at[0], one_r.at[0], me.partner)
    far_l = remote(docs, docv.at[me.core], one_s.at[1], one_r.at[1], me.partner)
    far_p = remote(plan, planv.at[me.core], one_s.at[2], one_r.at[2], me.partner)
    bits_in = pltpu.make_async_copy(bits, bitv, loc.at[3])
    for copy in (own_x, far_x, own_l, far_l, own_p, far_p, bits_in):
        copy.start()

    def k_src(j):
        return k.at[:, pl.ds(j * HEAD, HEAD)]

    def wide(ref, core, j):
        return ref.at[pl.ds(core * HALF, HALF), pl.ds(j * GROUP * HEAD, GROUP * HEAD)]

    spot = pl.multiple_of(BAND + me.ctx * TOK, TOK)
    half_spot = pl.multiple_of(me.ctx * HALF, HALF)

    for n in range(8):
        to, j = n // 4, n % 4
        push(me, k_src(j), kpad.at[pl.ds(spot, TOK), :], k_s.at[n], k_r.at[me.ctx], to, me.core * 4 + j)
    for n in range(16):
        landed(wfull.at[me.ylo, me.z, pl.ds(n * 16, 16), :], w_r.at[n])
    def piece(z, sub):
        ylo = me.ylo if sub < SUBS // 2 else 1 - me.ylo
        return wfull.at[ylo, z, pl.ds(sub % (SUBS // 2) * SUB_ROWS, SUB_ROWS), :]

    def ring(s, sub):
        z_up, z_dn = (me.z + N_Z - s) % N_Z, (me.z + s) % N_Z
        n = s * SUBS + sub
        up = remote(piece(z_up, sub), piece(z_up, sub), up_s.at[n], up_r.at[n], me.up)
        dn = remote(piece(z_dn, sub), piece(z_dn, sub), dn_s.at[n], dn_r.at[n], me.down)
        half = up if sub % 2 == 0 else dn
        return [up, dn] if s < 3 else [half]

    started = {}

    def go(s, sub):
        started[s, sub] = ring(s, sub)
        for copy in started[s, sub]:
            copy.start()

    for sub in range(SUBS // 2):
        go(0, sub)
    for n in range(8):
        to, j = n // 4, n % 4
        push(me, wide(q, to, j), qa.at[pl.ds(half_spot, HALF), :], q_s.at[n], q_r.at[me.ctx], to, me.core * 4 + j)
    for n in range(8):
        to, j = n // 4, n % 4
        push(me, wide(g, to, j), ga.at[pl.ds(half_spot, HALF), :], g_s.at[n], g_r.at[me.ctx], to, me.core * 4 + j)
    own_x.wait()
    far_x.wait()
    for n in range(16):
        landed(wfull.at[1 - me.ylo, me.z, pl.ds(n * 16, 16), :], w_r.at[16 + n])
    for sub in range(SUBS // 2, SUBS):
        go(0, sub)

    def project(z):
        for ylo in range(2):
            col = pl.multiple_of(ylo * 2048 + z * 256, 256)
            part = xv[:, :, pl.ds(col, 256)].reshape(2 * TOK, 256)
            vacc[...] += jnp.dot(part, wfull[ylo, z], preferred_element_type=F32)

    def transposed(out, pad):
        for b in range(2):
            for n in range(12):
                rows = pl.ds(pl.multiple_of(core * HALF + b * BLOCK + n * 128, BLOCK), 128)
                out[b, :, n * 128 : n * 128 + 128] = pad[rows, :].T

    def stacked(ref, i, b):
        rows = pl.ds(pl.multiple_of(i * HALF + b * BLOCK, BLOCK), BLOCK)
        return jnp.concatenate([ref[rows, h * HEAD : (h + 1) * HEAD] for h in range(GROUP)], axis=0)

    def unstack(ref, i, b, value):
        rows = pl.ds(pl.multiple_of(i * HALF + b * BLOCK, BLOCK), BLOCK)
        for h in range(GROUP):
            ref[rows, h * HEAD : (h + 1) * HEAD] = value[h * BLOCK : (h + 1) * BLOCK]

    def keys_of(i, b):
        block = i * 4 + core * 2 + b
        return block, pl.ds(pl.multiple_of(block * BLOCK, BLOCK), WIN)

    key_row = lax.broadcasted_iota(I32, (WIN, GROUP * BLOCK), 0)
    lane = lax.broadcasted_iota(I32, (1, GROUP * BLOCK), 1) % BLOCK

    def iota(shape, axis):
        return lax.broadcasted_iota(I32, shape, axis)

    def tables():
        doc = docv[par]
        first = jnp.zeros(doc.shape, I32)
        for d in range(15):
            size = jnp.sum(jnp.where(doc == d, 1, 0), axis=1, keepdims=True)
            first = first + jnp.where(doc > d, size, 0)
        first = jnp.broadcast_to(first, (SEQ // BLOCK, SEQ))
        mine = iota(first.shape, 0) == iota(first.shape, 1) // BLOCK
        same = iota((SEQ, GROUP * BLOCK), 0) % BLOCK == iota((SEQ, GROUP * BLOCK), 1) % BLOCK
        same = jnp.where(same, 1.0, 0.0).astype(BF)
        spread = []
        for part in (first // BLOCK, first % BLOCK):
            part = jnp.where(mine, part, 0).astype(F32).astype(BF)
            spread.append(jnp.dot(part, same, preferred_element_type=F32).astype(I32))
        firstv[...] = spread[0] * BLOCK + spread[1]

        plan = planv[par]
        block = iota((1, SEQ), 1) // BLOCK
        key_block, col = iota(tsv.shape, 0), iota(tsv.shape, 1)
        cand = col // BLOCK
        query_block = (key_block // 4 + cand // 2) * 4 + core * 2 + cand % 2
        place = jnp.zeros((1, SEQ), I32)
        step = jnp.zeros(tsv.shape, I32)
        for p in range(SEQ // BLOCK):
            at = plan[:, p : p + 1]
            place = place + jnp.where(block == at, p, 0)
            step = step + jnp.where(query_block == at, p // 4, 0) - jnp.where(key_block == at, p // 4, 0)
        step = jnp.where(step < 0, step + N_CTX, step)
        ahead = query_block - key_block
        seen = (cand < 10) & (query_block < SEQ // BLOCK) & (ahead >= 0) & (ahead <= BAND // BLOCK)
        tsv[...] = jnp.where(seen, step, -1)
        planrow[...] = place * BLOCK + iota((1, SEQ), 1) % BLOCK

    def scores(low, high):
        @pl.loop(low, high)
        def _(i):
            landed(qa.at[pl.ds(pl.multiple_of(i * HALF, HALF), HALF), :], q_r.at[i])
            for b in range(2):
                block, rows = keys_of(i, b)
                first = firstv[pl.ds(block, 1), :] + (BAND - block * BLOCK)
                allowed = (key_row >= first) & (key_row <= lane + BAND)
                s = lax.dot_general(kpad[rows, :], stacked(qa, i, b), NT, preferred_element_type=F32)
                s = jnp.where(allowed, s * (SCALE * LOG2E), NEG)
                weight = jnp.exp2(s - jnp.max(s, axis=0, keepdims=True))
                prob = weight * (1.0 / jnp.sum(weight, axis=0, keepdims=True))
                pst[i * 2 + b] = prob.astype(BF)

    for s in range(1, 4):
        for sub in range(SUBS):
            up, dn = started[s - 1, sub]
            up.wait_recv()
            dn.wait_recv()
            go(s, sub)
        project((me.z + N_Z - s + 1) % N_Z)
        if s > 1:
            project((me.z + s - 1) % N_Z)
    for i in range(N_CTX):
        landed(kpad.at[pl.ds(BAND + i * TOK, TOK), :], k_r.at[i])
    transposed(kt, kpad)
    for copy in (own_l, far_l, own_p, far_p):
        copy.wait()
    tables()
    project((me.z + N_Z - 3) % N_Z)
    project((me.z + 3) % N_Z)
    scores(0, 3)
    for sub in range(SUBS):
        started[3, sub][0].wait_recv()
    project((me.z + N_Z - 4) % N_Z)

    vbuf[...] = vacc[...].astype(BF)

    def v_src(p, jj):
        return vbuf.at[pl.ds(p * TOK, TOK), pl.ds(jj * HEAD, HEAD)]

    routes = [(n // 4, n // 2 % 2, n % 2) for n in range(8)]
    for n, (to, p, jj) in enumerate(routes):
        push(
            me, v_src(p, jj), vpad.at[pl.ds(spot, TOK), :], v_s.at[n], v_r.at[me.ctx], to, p * 4 + me.core * 2 + jj
        )
    scores(3, N_CTX)
    bits_in.wait()
    wanted = [bitv[pl.ds(t * 8 + f * 4 + me.head, 1), :] for f in range(2) for t in range(N_CTX)]
    jitter = (jnp.concatenate(wanted, axis=0).astype(F32) * 2.0**-30 - 0.5) * 2.0**-4
    parts = []
    for _ in range(3):
        parts.append(jitter.astype(BF))
        jitter = jitter - parts[-1].astype(F32)
    at = planrow[:, pl.ds(pl.multiple_of(core * (SEQ // 2), SEQ // 2), SEQ // 2)]
    there = lax.broadcasted_iota(I32, (SEQ, SEQ // 2), 0) == at
    moved = jnp.dot(
        jnp.concatenate(parts, axis=0), jnp.where(there, 1.0, 0.0).astype(BF), preferred_element_type=F32
    )
    moved = moved[0:16] + moved[16:32] + moved[32:48]
    jit[...] = jnp.concatenate([moved, jnp.zeros((112, SEQ // 2), F32)], axis=0).T
    for i in range(N_CTX):
        landed(vpad.at[pl.ds(BAND + i * TOK, TOK), :], v_r.at[i])
    transposed(vt, vpad)

    def out_wide(ref, j):
        cols = pl.ds(pl.multiple_of(j * GROUP * HEAD, HEAD), GROUP * HEAD)
        return ref.at[pl.ds(pl.multiple_of(me.core * HALF, HALF), HALF), cols]

    def home(ref, i):
        return ref.at[pl.ds(pl.multiple_of(i * HALF, HALF), HALF), :]

    @pl.loop(0, N_CTX)
    def _(i):
        landed(home(ga, i), g_r.at[i])
        window = pl.ds(pl.multiple_of(i * TOK, TOK), WIN)
        for b in range(2):
            n = i * 2 + b
            _, rows = keys_of(i, b)
            low, qs, gs = pst[n], stacked(qa, i, b), stacked(ga, i, b)
            out_t = jnp.dot(vt[b, :, window], low, preferred_element_type=F32).astype(BF).astype(F32)
            unstack(oc, i, b, out_t.T.astype(BF))
            delta = jnp.sum(gs.astype(F32).T * out_t, axis=0, keepdims=True)
            dprob = lax.dot_general(vpad[rows, :], gs, NT, preferred_element_type=F32)
            dscore = (low.astype(F32) * (dprob - delta)).astype(BF)
            dq_t = jnp.dot(kt[b, :, window], dscore, preferred_element_type=F32)
            unstack(dqc, i, b, (dq_t * SCALE).T.astype(BF))
            key_term = jnp.dot(dscore, qs, preferred_element_type=F32) * SCALE
            kvb[n, EDGE : EDGE + WIN, 0:HEAD] = key_term.astype(BF)
            kvb[n, EDGE : EDGE + WIN, HEAD:] = jnp.dot(low, gs, preferred_element_type=F32).astype(BF)
        push(me, home(oc, i), out_wide(att, me.head), o_s.at[i], o_r.at[me.core * 4 + me.head], me.par, i)

    def gather(out, half, n):
        tile_at = half * 4 + n

        @pl.loop(0, 4)
        def _(m):
            pieces = []
            for c in range(10):
                i, b = (tile_at + c // 2) % N_CTX, c % 2
                row = EDGE + BAND + (m - c // 2 * 4 - core * 2 - b) * BLOCK
                pieces.append(kvb[i * 2 + b, pl.ds(pl.multiple_of(row, BLOCK), BLOCK), :])
            pieces += pieces[0:2]
            step = tsv[pl.ds(tile_at * 4 + m, 1), :]
            pick = jnp.where(code[...] == step, 1.0, 0.0).astype(BF)
            sums = jnp.dot(pick, jnp.concatenate(pieces, axis=0), preferred_element_type=F32).astype(BF)
            dst = pl.ds(pl.multiple_of(n * TOK + m * BLOCK, BLOCK), BLOCK)
            for t in range(N_CTX):
                out[0, t, dst, :] = sums[t * BLOCK : (t + 1) * BLOCK, 0:HEAD]
                out[1, t, dst, :] = sums[t * BLOCK : (t + 1) * BLOCK, HEAD:]

    def rows_of(n):
        return pl.ds(n * TOK, TOK)

    swaps = []
    for n in range(4):
        gather(away_t, 1 - core, n)
        swaps.append(
            remote(away_t.at[:, :, rows_of(n), :], part.at[:, :, rows_of(n), :], sw_s.at[n], sw_r.at[n], me.partner)
        )
        swaps[n].start()

    def tile(ref, n):
        return ref.at[rows_of(n), :]

    v_core = me.head // 2
    v_col = pl.multiple_of(me.head % 2 * HEAD, HEAD)
    k_col = pl.multiple_of(me.head * HEAD, HEAD)
    v_dst = dv_pair.at[pl.ds(pl.multiple_of(me.par * TOK, TOK), TOK), pl.ds(v_col, HEAD)]
    k_dst = dko.at[:, pl.ds(k_col, HEAD)]
    for n in range(4):
        gather(own_t, core, n)
        swaps[n].wait_recv()

        @pl.loop(0, 2)
        def _(m, n=n):
            rows = pl.ds(pl.multiple_of(n * TOK + m * DROWS, DROWS), DROWS)
            noise = jit[rows, :]
            for f, out in ((0, kd), (1, vd)):
                acc = jnp.zeros((DROWS, HEAD), F32)
                for t in range(N_CTX):
                    total = acc + (own_t[f, t, rows, :].astype(F32) + part[f, t, rows, :].astype(F32))
                    u = noise[:, f * 8 + t : f * 8 + t + 1]
                    acc = (total + u * jnp.abs(total)).astype(BF).astype(F32)
                out[rows, :] = acc.astype(BF)

        push(me, tile(vd, n), v_dst, dv_s.at[n], dv_r.at[me.par * 2 + me.head % 2], v_core, me.core * 4 + n)
    for n in range(4):
        landed(dv_pair.at[pl.ds(n // 2 * TOK, TOK), pl.ds(n % 2 * HEAD, HEAD)], dv_r.at[n])

    def sub_ylo(sub):
        return 1 - me.ylo if sub == 0 else me.ylo

    def local_sum(z, ylo):
        col = pl.multiple_of(ylo * 2048 + z * 256, 256)
        return lax.dot_general(
            xv[:, :, pl.ds(col, 256)].reshape(2 * TOK, 256), dv_pair[...], TN, preferred_element_type=F32
        )

    ways = ((1, up_b, up_in, ru_s, ru_r, me.up), (-1, dn_b, dn_in, rd_s, rd_r, me.down))

    def sums(w, s, sub):
        _, buf, inn, ssem, rsem, to = ways[w]
        n = s * 2 + sub
        return remote(buf.at[n], inn.at[n], ssem.at[n], rsem.at[n], to)

    travel = {}

    def step(w, s, sub):
        sign, buf, inn = ways[w][:3]
        n = s * 2 + sub
        total = local_sum((me.z + N_Z + sign * (4 - s)) % N_Z, sub_ylo(sub))
        if (w, s - 1, sub) in travel:
            travel[w, s - 1, sub].wait_recv()
            total = total + inn[n - 2].astype(F32)
        buf[n] = total.astype(BF)
        travel[w, s, sub] = sums(w, s, sub)
        travel[w, s, sub].start()

    step(0, 0, 0)
    step(1, 0, 1)

    for i in range(N_CTX):
        push(me, home(dqc, i), out_wide(dqo, me.head), d_s.at[i], d_r.at[me.core * 4 + me.head], me.par, i)
    for n in range(4):
        push(me, tile(kd, n), k_dst, dk_s.at[n], dk_r.at[me.head], me.par, me.core * 4 + n)

    for s in range(1, 4):
        for sub in range(2):
            step(0, s, sub)
            step(1, s, sub)

    def finish(sub):
        total = local_sum(me.z, sub_ylo(sub))
        for w in range(2):
            travel[w, 3, sub].wait_recv()
            total = total + ways[w][2][6 + sub].astype(F32)
        c_b[sub] = total.astype(BF)

    def c_src(sub, n):
        return c_b.at[sub, pl.ds(n * 16, 16), :]

    far_in, near_in = c_in.at[me.core, N_CTX + me.ctx], c_in.at[me.core, me.ctx]
    mine = me.core * N_CTX + me.ctx
    finish(0)
    for n, (to, ctx) in enumerate(plane):
        remote(c_src(0, n), far_in, c_s.at[16 + n], c_r.at[16 + mine], me.over_there(to, ctx)).start()
    finish(1)
    for n, (to, ctx) in enumerate(plane):
        push(me, c_src(1, n), near_in, c_s.at[n], c_r.at[mine], to, ctx)
    for n in range(16):
        landed(c_in.at[n // N_CTX, N_CTX + n % N_CTX], c_r.at[16 + n])
    for n in range(16):
        landed(c_in.at[n // N_CTX, n % N_CTX], c_r.at[n])
    for half in range(2):
        total = c_in[half, 0].astype(F32)
        for i in range(1, 2 * N_CTX):
            total = total + c_in[half, i].astype(F32)
        wg[:, half * COLS : (half + 1) * COLS] = total

    for copies in started.values():
        for copy in copies:
            copy.wait_send()
    for n, (to, ctx) in enumerate(plane):
        pushed(me, w_src(to), w_s.at[n], to, ctx)
        remote(w_src(to), w_dst, w_s.at[16 + n], w_r.at[16 + n], me.over_there(to, ctx)).wait_send()
    for n in range(8):
        to, j = n // 4, n % 4
        pushed(me, k_src(j), k_s.at[n], to, me.core * 4 + j)
        pushed(me, wide(q, to, j), q_s.at[n], to, me.core * 4 + j)
        pushed(me, wide(g, to, j), g_s.at[n], to, me.core * 4 + j)
    for n, (to, p, jj) in enumerate(routes):
        pushed(me, v_src(p, jj), v_s.at[n], to, p * 4 + me.core * 2 + jj)
    for n in range(4):
        swaps[n].wait_send()
    for copy in travel.values():
        copy.wait_send()
    for n, (to, ctx) in enumerate(plane):
        pushed(me, c_src(1, n), c_s.at[n], to, ctx)
        remote(c_src(0, n), far_in, c_s.at[16 + n], c_r.at[16 + n], me.over_there(to, ctx)).wait_send()
    for n in range(4):
        pushed(me, tile(vd, n), dv_s.at[n], v_core, me.core * 4 + n)
        pushed(me, tile(kd, n), dk_s.at[n], me.par, me.core * 4 + n)
        landed(dko.at[:, pl.ds(n * HEAD, HEAD)], dk_r.at[n])
    for i in range(N_CTX):
        pushed(me, home(oc, i), o_s.at[i], me.par, i)
        pushed(me, home(dqc, i), d_s.at[i], me.par, i)
    for n in range(8):
        dst = (pl.ds(n // 4 * HALF, HALF), pl.ds(n % 4 * GROUP * HEAD, GROUP * HEAD))
        landed(att.at[dst], o_r.at[n])
        landed(dqo.at[dst], d_r.at[n])


def run(q, g, k, x, w, docs, plan, bits):
    slab = (256, COLS)
    rows = (SEQ // 2, GROUP * HEAD)
    table = (2, N_CTX, SEQ // 2, HEAD)
    return pl.pallas_call(
        kernel,
        out_shape=[
            jax.ShapeDtypeStruct((TOK, D), BF),
            jax.ShapeDtypeStruct((TOK, D), BF),
            jax.ShapeDtypeStruct((TOK, KVW), BF),
            jax.ShapeDtypeStruct((16, KVW), F32),
        ],
        in_specs=[ANY] * 8,
        out_specs=[ANY] * 3 + [pl.BlockSpec(memory_space=pltpu.VMEM)],
        scratch_shapes=[
            vmem((2, N_Z, 256, COLS), BF), vmem((2, TOK, D), BF), vmem((2 * TOK, COLS), BF), vmem((2 * TOK, COLS), F32),
            vmem(rows, BF), vmem(rows, BF), vmem(rows, BF), vmem(rows, BF),
            vmem((PAD_ROWS, HEAD), BF), vmem((PAD_ROWS, HEAD), BF), vmem((2, HEAD, 1536), BF), vmem((2, HEAD, 1536), BF),
            vmem((2,) + docs.shape, I32), vmem((2,) + plan.shape, I32), vmem(docs.shape, I32),
            vmem((SEQ // BLOCK, GROUP * BLOCK), I32),
            vmem(bits.shape, I32), vmem((SEQ // 2, HEAD), F32), vmem((SEQ // BLOCK, CAND * BLOCK), I32), vmem((N_CTX * BLOCK, CAND * BLOCK), I32),
            vmem((16, WIN, GROUP * BLOCK), BF), vmem((16, SPAN, 2 * HEAD), BF),
            vmem(table, BF), vmem(table, BF), vmem(table, BF),
            vmem((2 * TOK, COLS), BF), vmem((SEQ // 2, HEAD), BF), vmem((SEQ // 2, HEAD), BF),
            vmem((8,) + slab, BF), vmem((8,) + slab, BF), vmem((8,) + slab, BF), vmem((8,) + slab, BF),
            vmem((2,) + slab, BF), vmem((2, 2 * N_CTX, 16, COLS), BF),
            dma(32), dma(32), dma(8), dma(8), dma(8), dma(8), dma(8), dma(8), dma(8), dma(8),
            dma(6), dma(6), dma(4 * SUBS), dma(4 * SUBS), dma(4 * SUBS), dma(4 * SUBS), dma(5),
            dma(4), dma(4), dma(8), dma(8), dma(8), dma(8), dma(4), dma(4), dma(4), dma(4),
            dma(8), dma(8), dma(8), dma(8), dma(32), dma(32),
        ],
        compiler_params=pltpu.CompilerParams(
            collective_id=0, has_side_effects=True, vmem_limit_bytes=60 * 2**20
        ),
        cost_estimate=pl.CostEstimate(flops=6 * 10**9, bytes_accessed=16 * 2**20, transcendentals=2 * 10**6),
        name="cycle",
    )(q, g, k, x, w, docs, plan, bits)


def move_kernel(*refs):
    for n in range(4):
        refs[4 + n][...] = refs[n][...]


def move(arrays):
    steps = 2
    specs = [pl.BlockSpec((a.shape[0] // steps, a.shape[1]), lambda i: (i, 0)) for a in arrays]
    return pl.pallas_call(
        move_kernel,
        grid=(steps,),
        out_shape=[jax.ShapeDtypeStruct(a.shape, a.dtype) for a in arrays],
        in_specs=specs,
        out_specs=specs,
        compiler_params=pltpu.CompilerParams(vmem_limit_bytes=60 * 2**20),
        name="move",
    )(*arrays)


def local(queries, key_vectors, activations, value_weight, attended_grad, doc_ids, shard_plan, round_bits):
    bits = round_bits.transpose(0, 2, 1).reshape(N_CTX * 8, SEQ)
    outs = run(
        queries[0], attended_grad[0], key_vectors[0], activations[0], value_weight, doc_ids, shard_plan, bits
    )
    att, dqo, dko, wg = move(outs)
    return att[None], dqo[None], dko[None], wg


def solution(mesh):
    rows = P("dp", "ctx", None)
    every = P(("dp", "ctx"), None)
    return jax.shard_map(
        local,
        mesh=mesh,
        in_specs=(rows, rows, rows, every, rows, P("dp", None), P("dp", None), P()),
        out_specs=(rows, rows, rows, every),
        check_vma=False,
    )
```

```python
import functools

import jax
import jax.numpy as jnp
from jax import lax
from jax.experimental import pallas as pl
from jax.experimental.pallas import tpu as pltpu
from jax.sharding import PartitionSpec as P

MESH = pl.DeviceIdType.MESH
ANY = pl.BlockSpec(memory_space=pl.ANY)
BF = jnp.bfloat16
F32 = jnp.float32
I32 = jnp.int32

N_CTX = 8
N_Z = 8
HEAD = 128
GROUP = 8
TOK = 128
HALF = 64
SEQ = 1024
BLOCK = 32
BAND = 512
WIN = BAND + BLOCK
D = 4096
KVW = 512
COLS = 256
PAD_ROWS = SEQ + BAND + 128
SCALE = HEAD**-0.5
LOG2E = 1.4426950408889634
NEG = -1e30
SUBS = 2
SUB_ROWS = 512 // SUBS
DROWS = 64
EDGE = 3 * BLOCK
SPAN = WIN + 2 * EDGE
CAND = 12

NT = (((1,), (1,)), ((), ()))
TN = (((0,), (0,)), ((), ()))


def vmem(shape, dtype):
    return pltpu.VMEM(shape, dtype)


def dma(*shape):
    return pltpu.SemaphoreType.DMA(shape)


class Place:
    def __init__(self):
        self.dp = lax.axis_index("dp")
        self.ctx = lax.axis_index("ctx")
        self.core = self.dp % 2
        self.z = (self.dp // 2) % N_Z
        self.ylo = self.dp // 16
        self.base = self.dp - self.core
        self.par = self.ctx // 4
        self.head = self.ctx % 4
        self.partner = (self.base + 1 - self.core, self.ctx)
        self.up = (self.ylo * 16 + (self.z + 1) % N_Z * 2 + self.core, self.ctx)
        self.down = (self.ylo * 16 + (self.z + N_Z - 1) % N_Z * 2 + self.core, self.ctx)

    def over_there(self, core, ctx):
        return (self.base + 16 - 32 * self.ylo + core, jnp.int32(ctx))

    def is_me(self, core, ctx):
        return (self.core == core) & (self.ctx == ctx)


def greet(me):
    barrier = pltpu.get_barrier_semaphore()
    for ylo in range(2):
        for core in range(2):
            for ctx in range(N_CTX):

                @pl.when(jnp.logical_not((me.ylo == ylo) & me.is_me(core, ctx)))
                def _(ylo=ylo, core=core, ctx=ctx):
                    to = (ylo * 16 + me.z * 2 + core, jnp.int32(ctx))
                    pl.semaphore_signal(barrier, inc=1, device_id=to, device_id_type=MESH)

    for other in (me.up, me.down):
        pl.semaphore_signal(barrier, inc=1, device_id=other, device_id_type=MESH)
    pl.semaphore_wait(barrier, 4 * N_CTX + 1)


def remote(src, dst, ssem, rsem, device):
    return pltpu.make_async_remote_copy(
        src_ref=src, dst_ref=dst, send_sem=ssem, recv_sem=rsem, device_id=device, device_id_type=MESH
    )


def push(me, src, dst, ssem, rsem, core, ctx):
    mine = me.is_me(core, ctx)

    @pl.when(mine)
    def _():
        pltpu.make_async_copy(src, dst, rsem).start()

    @pl.when(jnp.logical_not(mine))
    def _():
        remote(src, dst, ssem, rsem, (me.base + core, jnp.int32(ctx))).start()


def pushed(me, src, ssem, core, ctx):
    @pl.when(jnp.logical_not(me.is_me(core, ctx)))
    def _():
        remote(src, src, ssem, ssem, (me.base + core, jnp.int32(ctx))).wait_send()


def landed(dst, rsem):
    pltpu.make_async_copy(dst, dst, rsem).wait()


def kernel(
    q, g, k, x, w, docs, plan, bits, att, dqo, dko, wg,
    wfull, xv, vbuf, vacc, qa, ga, oc, dqc, kpad, vpad, kt, vt, docv, planv, planrow, firstv, bitv, jit,
    tsv, code, pst, kvb, away_t, own_t, part, dv_pair, kd, vd,
    up_b, dn_b, up_in, dn_in, c_b, c_in,
    w_s, w_r, q_s, q_r, g_s, g_r, k_s, k_r, v_s, v_r, one_s, one_r, up_s, up_r, dn_s, dn_r, loc,
    sw_s, sw_r, o_s, o_r, d_s, d_r, dk_s, dk_r, dv_s, dv_r, ru_s, ru_r, rd_s, rd_r, c_s, c_r,
):
    me = Place()
    core, par = me.core, me.par
    for pad in (kpad, vpad):
        pad[0:BAND, :] = jnp.zeros((BAND, HEAD), BF)
        pad[BAND + SEQ :, :] = jnp.zeros((PAD_ROWS - BAND - SEQ, HEAD), BF)
    kvb[:, 0:EDGE, :] = jnp.zeros((16, EDGE, 2 * HEAD), BF)
    kvb[:, EDGE + WIN :, :] = jnp.zeros((16, EDGE, 2 * HEAD), BF)
    down = lax.broadcasted_iota(I32, code.shape, 0)
    right = lax.broadcasted_iota(I32, code.shape, 1)
    code[...] = jnp.where(down % BLOCK == right % BLOCK, down // BLOCK, N_CTX)
    vacc[...] = jnp.zeros_like(vacc)
    greet(me)
    plane = [(n // N_CTX, n % N_CTX) for n in range(2 * N_CTX)]

    def w_src(core):
        return w.at[:, pl.ds(core * COLS, COLS)]

    row = pl.multiple_of(me.core * 128 + me.ctx * 16, 16)
    w_dst = wfull.at[me.ylo, me.z, pl.ds(row, 16), :]
    for n, (to, ctx) in enumerate(plane):
        push(me, w_src(to), w_dst, w_s.at[n], w_r.at[me.core * N_CTX + me.ctx], to, ctx)
    for n, (to, ctx) in enumerate(plane):
        remote(w_src(to), w_dst, w_s.at[16 + n], w_r.at[16 + me.core * N_CTX + me.ctx], me.over_there(to, ctx)).start()

    own_x = pltpu.make_async_copy(x, xv.at[me.core], loc.at[0])
    own_l = pltpu.make_async_copy(docs, docv.at[me.core], loc.at[1])
    own_p = pltpu.make_async_copy(plan, planv.at[me.core], loc.at[2])
    far_x = remote(x, xv.at[me.core], one_s.at[0], one_r.at[0], me.partner)
    far_l = remote(docs, docv.at[me.core], one_s.at[1], one_r.at[1], me.partner)
    far_p = remote(plan, planv.at[me.core], one_s.at[2], one_r.at[2], me.partner)
    bits_in = pltpu.make_async_copy(bits, bitv, loc.at[3])
    for copy in (own_x, far_x, own_l, far_l, own_p, far_p, bits_in):
        copy.start()

    def turned(n):
        return (n + me.ctx) % N_CTX

    def k_src(j):
        return k.at[:, pl.ds(pl.multiple_of(j * HEAD, HEAD), HEAD)]

    def wide(ref, core, j):
        cols = pl.ds(pl.multiple_of(j * GROUP * HEAD, HEAD), GROUP * HEAD)
        return ref.at[pl.ds(pl.multiple_of(core * HALF, HALF), HALF), cols]

    spot = pl.multiple_of(BAND + me.ctx * TOK, TOK)
    half_spot = pl.multiple_of(me.ctx * HALF, HALF)

    for n in range(8):
        to, j = turned(n) // 4, turned(n) % 4
        push(me, k_src(j), kpad.at[pl.ds(spot, TOK), :], k_s.at[n], k_r.at[me.ctx], to, me.core * 4 + j)
    for n in range(16):
        landed(wfull.at[me.ylo, me.z, pl.ds(n * 16, 16), :], w_r.at[n])
    def piece(z, sub):
        ylo = me.ylo if sub < SUBS // 2 else 1 - me.ylo
        return wfull.at[ylo, z, pl.ds(sub % (SUBS // 2) * SUB_ROWS, SUB_ROWS), :]

    def ring(s, sub):
        z_up, z_dn = (me.z + N_Z - s) % N_Z, (me.z + s) % N_Z
        n = s * SUBS + sub
        up = remote(piece(z_up, sub), piece(z_up, sub), up_s.at[n], up_r.at[n], me.up)
        dn = remote(piece(z_dn, sub), piece(z_dn, sub), dn_s.at[n], dn_r.at[n], me.down)
        half = up if sub % 2 == 0 else dn
        return [up, dn] if s < 3 else [half]

    started = {}

    def go(s, sub):
        started[s, sub] = ring(s, sub)
        for copy in started[s, sub]:
            copy.start()

    for sub in range(SUBS // 2):
        go(0, sub)
    own_x.wait()
    far_x.wait()
    for n in range(16):
        landed(wfull.at[1 - me.ylo, me.z, pl.ds(n * 16, 16), :], w_r.at[16 + n])
    for sub in range(SUBS // 2, SUBS):
        go(0, sub)

    for n in range(8):
        to, j = turned(n) // 4, turned(n) % 4
        push(me, wide(q, to, j), qa.at[pl.ds(half_spot, HALF), :], q_s.at[n], q_r.at[me.ctx], to, me.core * 4 + j)
    for n in range(8):
        to, j = turned(n) // 4, turned(n) % 4
        push(me, wide(g, to, j), ga.at[pl.ds(half_spot, HALF), :], g_s.at[n], g_r.at[me.ctx], to, me.core * 4 + j)
    def project(z):
        for ylo in range(2):
            col = pl.multiple_of(ylo * 2048 + z * 256, 256)
            part = xv[:, :, pl.ds(col, 256)].reshape(2 * TOK, 256)
            vacc[...] += jnp.dot(part, wfull[ylo, z], preferred_element_type=F32)

    def transposed(out, pad):
        for b in range(2):
            for n in range(12):
                rows = pl.ds(pl.multiple_of(core * HALF + b * BLOCK + n * 128, BLOCK), 128)
                out[b, :, n * 128 : n * 128 + 128] = pad[rows, :].T

    def stacked(ref, i, b):
        rows = pl.ds(pl.multiple_of(i * HALF + b * BLOCK, BLOCK), BLOCK)
        return jnp.concatenate([ref[rows, h * HEAD : (h + 1) * HEAD] for h in range(GROUP)], axis=0)

    def unstack(ref, i, b, value):
        rows = pl.ds(pl.multiple_of(i * HALF + b * BLOCK, BLOCK), BLOCK)
        for h in range(GROUP):
            ref[rows, h * HEAD : (h + 1) * HEAD] = value[h * BLOCK : (h + 1) * BLOCK]

    def keys_of(i, b):
        block = i * 4 + core * 2 + b
        return block, pl.ds(pl.multiple_of(block * BLOCK, BLOCK), WIN)

    key_row = lax.broadcasted_iota(I32, (WIN, GROUP * BLOCK), 0)
    lane = lax.broadcasted_iota(I32, (1, GROUP * BLOCK), 1) % BLOCK

    def iota(shape, axis):
        return lax.broadcasted_iota(I32, shape, axis)

    def tables():
        doc = docv[par]
        first = jnp.zeros(doc.shape, I32)
        for d in range(15):
            size = jnp.sum(jnp.where(doc == d, 1, 0), axis=1, keepdims=True)
            first = first + jnp.where(doc > d, size, 0)
        first = jnp.broadcast_to(first, (SEQ // BLOCK, SEQ))
        mine = iota(first.shape, 0) == iota(first.shape, 1) // BLOCK
        same = iota((SEQ, GROUP * BLOCK), 0) % BLOCK == iota((SEQ, GROUP * BLOCK), 1) % BLOCK
        same = jnp.where(same, 1.0, 0.0).astype(BF)
        spread = []
        for part in (first // BLOCK, first % BLOCK):
            part = jnp.where(mine, part, 0).astype(F32).astype(BF)
            spread.append(jnp.dot(part, same, preferred_element_type=F32).astype(I32))
        firstv[...] = spread[0] * BLOCK + spread[1]

        plan = planv[par]
        block = iota((1, SEQ), 1) // BLOCK
        key_block, col = iota(tsv.shape, 0), iota(tsv.shape, 1)
        cand = col // BLOCK
        query_block = (key_block // 4 + cand // 2) * 4 + core * 2 + cand % 2
        place = jnp.zeros((1, SEQ), I32)
        step = jnp.zeros(tsv.shape, I32)
        for p in range(SEQ // BLOCK):
            at = plan[:, p : p + 1]
            place = place + jnp.where(block == at, p, 0)
            step = step + jnp.where(query_block == at, p // 4, 0) - jnp.where(key_block == at, p // 4, 0)
        step = jnp.where(step < 0, step + N_CTX, step)
        ahead = query_block - key_block
        seen = (cand < 10) & (query_block < SEQ // BLOCK) & (ahead >= 0) & (ahead <= BAND // BLOCK)
        tsv[...] = jnp.where(seen, step, -1)
        planrow[...] = place * BLOCK + iota((1, SEQ), 1) % BLOCK

    def scores(low, high):
        @pl.loop(low, high)
        def _(i):
            landed(qa.at[pl.ds(pl.multiple_of(i * HALF, HALF), HALF), :], q_r.at[i])
            for b in range(2):
                block, rows = keys_of(i, b)
                first = firstv[pl.ds(block, 1), :] + (BAND - block * BLOCK)
                allowed = (key_row >= first) & (key_row <= lane + BAND)
                s = lax.dot_general(kpad[rows, :], stacked(qa, i, b), NT, preferred_element_type=F32)
                s = jnp.where(allowed, s * (SCALE * LOG2E), NEG)
                weight = jnp.exp2(s - jnp.max(s, axis=0, keepdims=True))
                prob = weight * (1.0 / jnp.sum(weight, axis=0, keepdims=True))
                pst[i * 2 + b] = prob.astype(BF)

    def order(s, sub):
        up, dn = started[s - 1, sub]
        return (up, dn) if sub % 2 == 0 else (dn, up)

    for s in range(1, 4):
        for sub in range(SUBS):
            started[s, sub] = ring(s, sub)
            first, second = started[s - 1, sub] if s < 3 else order(s, sub)
            first.wait_recv()
            started[s, sub][0].start()
            second.wait_recv()
            for copy in started[s, sub][1:]:
                copy.start()
        project((me.z + N_Z - s + 1) % N_Z)
        if s > 1:
            project((me.z + s - 1) % N_Z)
    for i in range(N_CTX):
        landed(kpad.at[pl.ds(BAND + i * TOK, TOK), :], k_r.at[i])
    transposed(kt, kpad)
    for copy in (own_l, far_l, own_p, far_p):
        copy.wait()
    tables()
    project((me.z + N_Z - 3) % N_Z)
    project((me.z + 3) % N_Z)
    scores(0, 3)
    for sub in range(SUBS):
        started[3, sub][0].wait_recv()
    project((me.z + N_Z - 4) % N_Z)

    vbuf[...] = vacc[...].astype(BF)

    def v_src(p, jj):
        return vbuf.at[pl.ds(p * TOK, TOK), pl.ds(jj * HEAD, HEAD)]

    routes = [(n // 4, n // 2 % 2, n % 2) for n in range(8)]
    for n, (to, p, jj) in enumerate(routes):
        push(
            me, v_src(p, jj), vpad.at[pl.ds(spot, TOK), :], v_s.at[n], v_r.at[me.ctx], to, p * 4 + me.core * 2 + jj
        )
    scores(3, N_CTX)
    bits_in.wait()
    wanted = [bitv[pl.ds(t * 8 + f * 4 + me.head, 1), :] for f in range(2) for t in range(N_CTX)]
    jitter = (jnp.concatenate(wanted, axis=0).astype(F32) * 2.0**-30 - 0.5) * 2.0**-4
    parts = []
    for _ in range(3):
        parts.append(jitter.astype(BF))
        jitter = jitter - parts[-1].astype(F32)
    at = planrow[:, pl.ds(pl.multiple_of(core * (SEQ // 2), SEQ // 2), SEQ // 2)]
    there = lax.broadcasted_iota(I32, (SEQ, SEQ // 2), 0) == at
    moved = jnp.dot(
        jnp.concatenate(parts, axis=0), jnp.where(there, 1.0, 0.0).astype(BF), preferred_element_type=F32
    )
    moved = moved[0:16] + moved[16:32] + moved[32:48]
    jit[...] = jnp.concatenate([moved, jnp.zeros((112, SEQ // 2), F32)], axis=0).T
    for i in range(N_CTX):
        landed(vpad.at[pl.ds(BAND + i * TOK, TOK), :], v_r.at[i])
    transposed(vt, vpad)

    def out_wide(ref, j):
        cols = pl.ds(pl.multiple_of(j * GROUP * HEAD, HEAD), GROUP * HEAD)
        return ref.at[pl.ds(pl.multiple_of(me.core * HALF, HALF), HALF), cols]

    def home(ref, i):
        return ref.at[pl.ds(pl.multiple_of(i * HALF, HALF), HALF), :]

    @pl.loop(0, N_CTX)
    def _(i):
        landed(home(ga, i), g_r.at[i])
        window = pl.ds(pl.multiple_of(i * TOK, TOK), WIN)
        for b in range(2):
            n = i * 2 + b
            _, rows = keys_of(i, b)
            low, qs, gs = pst[n], stacked(qa, i, b), stacked(ga, i, b)
            out_t = jnp.dot(vt[b, :, window], low, preferred_element_type=F32).astype(BF).astype(F32)
            unstack(oc, i, b, out_t.T.astype(BF))
            delta = jnp.sum(gs.astype(F32).T * out_t, axis=0, keepdims=True)
            dprob = lax.dot_general(vpad[rows, :], gs, NT, preferred_element_type=F32)
            dscore = (low.astype(F32) * (dprob - delta)).astype(BF)
            dq_t = jnp.dot(kt[b, :, window], dscore, preferred_element_type=F32)
            unstack(dqc, i, b, (dq_t * SCALE).T.astype(BF))
            key_term = jnp.dot(dscore, qs, preferred_element_type=F32) * SCALE
            kvb[n, EDGE : EDGE + WIN, 0:HEAD] = key_term.astype(BF)
            kvb[n, EDGE : EDGE + WIN, HEAD:] = jnp.dot(low, gs, preferred_element_type=F32).astype(BF)
        push(me, home(oc, i), out_wide(att, me.head), o_s.at[i], o_r.at[me.core * 4 + me.head], me.par, i)

    def gather(out, half, n):
        tile_at = half * 4 + n

        @pl.loop(0, 4)
        def _(m):
            pieces = []
            for c in range(10):
                i, b = (tile_at + c // 2) % N_CTX, c % 2
                row = EDGE + BAND + (m - c // 2 * 4 - core * 2 - b) * BLOCK
                pieces.append(kvb[i * 2 + b, pl.ds(pl.multiple_of(row, BLOCK), BLOCK), :])
            pieces += pieces[0:2]
            step = tsv[pl.ds(tile_at * 4 + m, 1), :]
            pick = jnp.where(code[...] == step, 1.0, 0.0).astype(BF)
            sums = jnp.dot(pick, jnp.concatenate(pieces, axis=0), preferred_element_type=F32).astype(BF)
            dst = pl.ds(pl.multiple_of(n * TOK + m * BLOCK, BLOCK), BLOCK)
            for t in range(N_CTX):
                out[0, t, dst, :] = sums[t * BLOCK : (t + 1) * BLOCK, 0:HEAD]
                out[1, t, dst, :] = sums[t * BLOCK : (t + 1) * BLOCK, HEAD:]

    def rows_of(n):
        return pl.ds(n * TOK, TOK)

    swaps = []
    for n in range(4):
        gather(away_t, 1 - core, n)
        swaps.append(
            remote(away_t.at[:, :, rows_of(n), :], part.at[:, :, rows_of(n), :], sw_s.at[n], sw_r.at[n], me.partner)
        )
        swaps[n].start()

    def tile(ref, n):
        return ref.at[rows_of(n), :]

    v_core = me.head // 2
    v_col = pl.multiple_of(me.head % 2 * HEAD, HEAD)
    k_col = pl.multiple_of(me.head * HEAD, HEAD)
    v_dst = dv_pair.at[pl.ds(pl.multiple_of(me.par * TOK, TOK), TOK), pl.ds(v_col, HEAD)]
    k_dst = dko.at[:, pl.ds(k_col, HEAD)]
    for n in range(4):
        gather(own_t, core, n)
        swaps[n].wait_recv()

        @pl.loop(0, 2)
        def _(m, n=n):
            rows = pl.ds(pl.multiple_of(n * TOK + m * DROWS, DROWS), DROWS)
            noise = jit[rows, :]
            for f, out in ((0, kd), (1, vd)):
                acc = jnp.zeros((DROWS, HEAD), F32)
                for t in range(N_CTX):
                    total = acc + (own_t[f, t, rows, :].astype(F32) + part[f, t, rows, :].astype(F32))
                    u = noise[:, f * 8 + t : f * 8 + t + 1]
                    acc = (total + u * jnp.abs(total)).astype(BF).astype(F32)
                out[rows, :] = acc.astype(BF)

        push(me, tile(vd, n), v_dst, dv_s.at[n], dv_r.at[me.par * 2 + me.head % 2], v_core, me.core * 4 + n)
    for n in range(4):
        landed(dv_pair.at[pl.ds(n // 2 * TOK, TOK), pl.ds(n % 2 * HEAD, HEAD)], dv_r.at[n])

    def sub_ylo(sub):
        return 1 - me.ylo if sub == 0 else me.ylo

    def local_sum(z, ylo):
        col = pl.multiple_of(ylo * 2048 + z * 256, 256)
        return lax.dot_general(
            xv[:, :, pl.ds(col, 256)].reshape(2 * TOK, 256), dv_pair[...], TN, preferred_element_type=F32
        )

    ways = ((1, up_b, up_in, ru_s, ru_r, me.up), (-1, dn_b, dn_in, rd_s, rd_r, me.down))

    def sums(w, s, sub):
        _, buf, inn, ssem, rsem, to = ways[w]
        n = s * 2 + sub
        return remote(buf.at[n], inn.at[n], ssem.at[n], rsem.at[n], to)

    travel = {}

    def step(w, s, sub):
        sign, buf, inn = ways[w][:3]
        n = s * 2 + sub
        total = local_sum((me.z + N_Z + sign * (4 - s)) % N_Z, sub_ylo(sub))
        if (w, s - 1, sub) in travel:
            travel[w, s - 1, sub].wait_recv()
            total = total + inn[n - 2].astype(F32)
        buf[n] = total.astype(BF)
        travel[w, s, sub] = sums(w, s, sub)
        travel[w, s, sub].start()

    step(0, 0, 0)
    step(1, 0, 1)


    for s in range(1, 4):
        for sub in range(2):
            step(0, s, sub)
            step(1, s, sub)
        if s == 1:
            for i in range(N_CTX):
                push(me, home(dqc, turned(i)), out_wide(dqo, me.head), d_s.at[i], d_r.at[me.core * 4 + me.head], me.par, turned(i))
            for n in range(4):
                push(me, tile(kd, n), k_dst, dk_s.at[n], dk_r.at[me.head], me.par, me.core * 4 + n)

    def finish(sub):
        total = local_sum(me.z, sub_ylo(sub))
        for w in range(2):
            travel[w, 3, sub].wait_recv()
            total = total + ways[w][2][6 + sub].astype(F32)
        c_b[sub] = total.astype(BF)

    def c_src(sub, n):
        return c_b.at[sub, pl.ds(n * 16, 16), :]

    far_in, near_in = c_in.at[me.core, N_CTX + me.ctx], c_in.at[me.core, me.ctx]
    mine = me.core * N_CTX + me.ctx
    finish(0)
    for n, (to, ctx) in enumerate(plane):
        remote(c_src(0, n), far_in, c_s.at[16 + n], c_r.at[16 + mine], me.over_there(to, ctx)).start()
    finish(1)
    for n, (to, ctx) in enumerate(plane):
        push(me, c_src(1, n), near_in, c_s.at[n], c_r.at[mine], to, ctx)
    for n in range(16):
        landed(c_in.at[n // N_CTX, N_CTX + n % N_CTX], c_r.at[16 + n])
    for n in range(16):
        landed(c_in.at[n // N_CTX, n % N_CTX], c_r.at[n])
    for half in range(2):
        total = c_in[half, 0].astype(F32)
        for i in range(1, 2 * N_CTX):
            total = total + c_in[half, i].astype(F32)
        wg[:, half * COLS : (half + 1) * COLS] = total

    for copies in started.values():
        for copy in copies:
            copy.wait_send()
    for n, (to, ctx) in enumerate(plane):
        pushed(me, w_src(to), w_s.at[n], to, ctx)
        remote(w_src(to), w_dst, w_s.at[16 + n], w_r.at[16 + n], me.over_there(to, ctx)).wait_send()
    for n in range(8):
        to, j = turned(n) // 4, turned(n) % 4
        pushed(me, k_src(j), k_s.at[n], to, me.core * 4 + j)
        pushed(me, wide(q, to, j), q_s.at[n], to, me.core * 4 + j)
        pushed(me, wide(g, to, j), g_s.at[n], to, me.core * 4 + j)
    for n, (to, p, jj) in enumerate(routes):
        pushed(me, v_src(p, jj), v_s.at[n], to, p * 4 + me.core * 2 + jj)
    for n in range(4):
        swaps[n].wait_send()
    for copy in travel.values():
        copy.wait_send()
    for n, (to, ctx) in enumerate(plane):
        pushed(me, c_src(1, n), c_s.at[n], to, ctx)
        remote(c_src(0, n), far_in, c_s.at[16 + n], c_r.at[16 + n], me.over_there(to, ctx)).wait_send()
    for n in range(4):
        pushed(me, tile(vd, n), dv_s.at[n], v_core, me.core * 4 + n)
        pushed(me, tile(kd, n), dk_s.at[n], me.par, me.core * 4 + n)
        landed(dko.at[:, pl.ds(n * HEAD, HEAD)], dk_r.at[n])
    for i in range(N_CTX):
        pushed(me, home(oc, i), o_s.at[i], me.par, i)
        pushed(me, home(dqc, turned(i)), d_s.at[i], me.par, turned(i))
    for n in range(8):
        dst = (pl.ds(n // 4 * HALF, HALF), pl.ds(n % 4 * GROUP * HEAD, GROUP * HEAD))
        landed(att.at[dst], o_r.at[n])
        landed(dqo.at[dst], d_r.at[n])


def run(q, g, k, x, w, docs, plan, bits):
    slab = (256, COLS)
    rows = (SEQ // 2, GROUP * HEAD)
    table = (2, N_CTX, SEQ // 2, HEAD)
    return pl.pallas_call(
        kernel,
        out_shape=[
            jax.ShapeDtypeStruct((TOK, D), BF),
            jax.ShapeDtypeStruct((TOK, D), BF),
            jax.ShapeDtypeStruct((TOK, KVW), BF),
            jax.ShapeDtypeStruct((16, KVW), F32),
        ],
        in_specs=[ANY] * 8,
        out_specs=[ANY] * 3 + [pl.BlockSpec(memory_space=pltpu.VMEM)],
        scratch_shapes=[
            vmem((2, N_Z, 256, COLS), BF), vmem((2, TOK, D), BF), vmem((2 * TOK, COLS), BF), vmem((2 * TOK, COLS), F32),
            vmem(rows, BF), vmem(rows, BF), vmem(rows, BF), vmem(rows, BF),
            vmem((PAD_ROWS, HEAD), BF), vmem((PAD_ROWS, HEAD), BF), vmem((2, HEAD, 1536), BF), vmem((2, HEAD, 1536), BF),
            vmem((2,) + docs.shape, I32), vmem((2,) + plan.shape, I32), vmem(docs.shape, I32),
            vmem((SEQ // BLOCK, GROUP * BLOCK), I32),
            vmem(bits.shape, I32), vmem((SEQ // 2, HEAD), F32), vmem((SEQ // BLOCK, CAND * BLOCK), I32), vmem((N_CTX * BLOCK, CAND * BLOCK), I32),
            vmem((16, WIN, GROUP * BLOCK), BF), vmem((16, SPAN, 2 * HEAD), BF),
            vmem(table, BF), vmem(table, BF), vmem(table, BF),
            vmem((2 * TOK, COLS), BF), vmem((SEQ // 2, HEAD), BF), vmem((SEQ // 2, HEAD), BF),
            vmem((8,) + slab, BF), vmem((8,) + slab, BF), vmem((8,) + slab, BF), vmem((8,) + slab, BF),
            vmem((2,) + slab, BF), vmem((2, 2 * N_CTX, 16, COLS), BF),
            dma(32), dma(32), dma(8), dma(8), dma(8), dma(8), dma(8), dma(8), dma(8), dma(8),
            dma(6), dma(6), dma(4 * SUBS), dma(4 * SUBS), dma(4 * SUBS), dma(4 * SUBS), dma(5),
            dma(4), dma(4), dma(8), dma(8), dma(8), dma(8), dma(4), dma(4), dma(4), dma(4),
            dma(8), dma(8), dma(8), dma(8), dma(32), dma(32),
        ],
        compiler_params=pltpu.CompilerParams(
            collective_id=0, has_side_effects=True, vmem_limit_bytes=60 * 2**20
        ),
        cost_estimate=pl.CostEstimate(flops=6 * 10**9, bytes_accessed=16 * 2**20, transcendentals=2 * 10**6),
        name="cycle",
    )(q, g, k, x, w, docs, plan, bits)


def move_kernel(*refs):
    for n in range(4):
        refs[4 + n][...] = refs[n][...]


def move(arrays):
    steps = 2
    specs = [pl.BlockSpec((a.shape[0] // steps, a.shape[1]), lambda i: (i, 0)) for a in arrays]
    return pl.pallas_call(
        move_kernel,
        grid=(steps,),
        out_shape=[jax.ShapeDtypeStruct(a.shape, a.dtype) for a in arrays],
        in_specs=specs,
        out_specs=specs,
        compiler_params=pltpu.CompilerParams(vmem_limit_bytes=60 * 2**20),
        name="move",
    )(*arrays)


def local(queries, key_vectors, activations, value_weight, attended_grad, doc_ids, shard_plan, round_bits):
    bits = round_bits.transpose(0, 2, 1).reshape(N_CTX * 8, SEQ)
    outs = run(
        queries[0], attended_grad[0], key_vectors[0], activations[0], value_weight, doc_ids, shard_plan, bits
    )
    att, dqo, dko, wg = move(outs)
    return att[None], dqo[None], dko[None], wg


def solution(mesh):
    rows = P("dp", "ctx", None)
    every = P(("dp", "ctx"), None)
    return jax.shard_map(
        local,
        mesh=mesh,
        in_specs=(rows, rows, rows, every, rows, P("dp", None), P("dp", None), P()),
        out_specs=(rows, rows, rows, every),
        check_vma=False,
    )
```
